128 devices in a mesh: outer: 32 (over z, y, core), grp: 4 (over x).
Axes of the slice: x: 4, y: 4, z: 4, core: 2. Of those that a mesh axis runs over, the one named last changes fastest.
Arguments:
- link_ids: int32 [98304, 8], P(('outer', 'grp')), may hold values from 0 to 98303, as said below
- path_states: bfloat16 [98304, 8, 128], P(('outer', 'grp')), may hold values from -1 to 1
- final_grad: bfloat16 [98304, 128], P(('outer', 'grp')), may hold values from -6 to 6
- link_states: bfloat16 [98304, 128], P(('outer', 'grp')), may hold values from -6 to 6
- agg_grad: bfloat16 [98304, 128], P(('outer', 'grp')), may hold values from -3 to 3
- w_in: bfloat16 [128, 384], replicated, may hold values from -0.5 to 0.5
- w_rec: bfloat16 [128, 384], replicated, may hold values from -0.5 to 0.5
- b_in: float32 [384], replicated, may hold values from -1 to 1
- b_rec: float32 [384], replicated, may hold values from -1 to 1
Outputs:
- path_grad: bfloat16 [98304, 128], P(('outer', 'grp'))
- link_grad: float32 [98304, 128], P(('outer', 'grp'))
- w_in_grad: float32 [128, 384], replicated
- w_rec_grad: float32 [128, 384], replicated
- b_in_grad: float32 [384], replicated
- b_rec_grad: float32 [384], replicated
The draws below stay inside these ranges and needn't reach their ends.
Inputs may be any that keep to these rules, and one draw needn't show every extreme that they name: `link_ids`: within the 6144 hops of each device's paths (aligned blocks), at most 72 lie on links of any one owner (owner = id // 768), and exactly 72 for some owner in every block.
All inputs are finite; a program needn't handle non-finite values.
Results may differ from the reference program's by a relative error of at most 0.0035.
Values may be sent and summed in bfloat16 or wider, within the bound.
A program may use at most 128 MiB of HBM per device.

```python
import math
import jax
import jax.numpy as jnp
from jax import lax

S = 128
HOPS = 8
PATH_DEV = 768
LINK_DEV = 768
OWNERS = 128
PATHS = 98304
LINKS = 98304


def draw_link_ids(key, part):
    row_count = PATH_DEV * HOPS
    share = row_count // OWNERS
    half_share = share // 2
    hot_count = max(OWNERS // 8, 1)

    def one_block(block_key):
        key_perm, key_rows, key_local = jax.random.split(block_key, 3)
        ranking = jax.random.permutation(key_perm, OWNERS)
        placed = jnp.zeros((OWNERS,), jnp.int32).at[ranking].set(jnp.arange(OWNERS, dtype=jnp.int32))
        is_hot = (placed < hot_count).astype(jnp.int32)
        is_cold = ((placed >= hot_count) & (placed < 2 * hot_count)).astype(jnp.int32)
        counts = share + half_share * is_hot - half_share * is_cold
        ends = jnp.cumsum(counts)
        owners = jnp.searchsorted(ends, jnp.arange(row_count, dtype=jnp.int32), side='right').astype(jnp.int32)
        owners = jax.random.permutation(key_rows, owners)
        local_ids = jax.random.randint(key_local, (row_count,), 0, LINK_DEV, dtype=jnp.int32)
        return (owners * LINK_DEV + local_ids).astype(jnp.int32)
    block_keys = jax.random.split(key, OWNERS)
    every = jax.vmap(one_block)(block_keys)
    return every.reshape(PATH_DEV * OWNERS, HOPS)


def block_scale(key, extent, shards, smallest, top_value):
    factor_of, own = 1.0, jax.random.fold_in(key, 6)
    for position, shards_of in shards:
        draws = jnp.exp(jax.random.uniform(jax.random.fold_in(own, position), (shards_of,), jnp.float32, smallest / len(shards), top_value / len(shards)))
        factor_of = factor_of * jnp.repeat(draws, extent[position] // shards_of).reshape([-1 if axis == position else 1 for axis in range(len(extent))])
    return factor_of


def gaussian(stream_key, shape, deviation, bound, shards=(), kind=jnp.bfloat16):
    factor_of = block_scale(stream_key, shape, shards, -0.22, 0.18) if shards else 1.0
    result = jax.random.normal(stream_key, shape, jnp.float32) * deviation * factor_of
    return jnp.minimum(jnp.maximum(result, -bound), bound).astype(kind)


def setup_inputs(seed: int = 0) -> dict:
    streams_of = jax.random.split(jax.random.key(seed), 10)
    return {
        "link_ids": draw_link_ids(jax.random.fold_in(streams_of[9], 71), 0),
        "path_states": jnp.clip(jax.random.uniform(streams_of[1], (PATHS, HOPS, S), jnp.float32, -1.0, 1.0) * block_scale(streams_of[1], (PATHS, HOPS, S), ((0, 128),), -0.4, 0.0), -1.0, 1.0).astype(jnp.bfloat16),
        "final_grad": gaussian(streams_of[2], (PATHS, S), 1.0, 6.0, ((0, 128),)),
        "link_states": gaussian(streams_of[3], (LINKS, S), 1.0, 6.0, ((0, 128),)),
        "agg_grad": gaussian(streams_of[4], (LINKS, S), 0.5, 3.0, ((0, 128),)),
        "w_in": gaussian(streams_of[5], (S, 3 * S), S ** -0.5, 0.5),
        "w_rec": gaussian(streams_of[6], (S, 3 * S), S ** -0.5, 0.5),
        "b_in": jnp.clip(jax.random.uniform(streams_of[7], (3 * S,), jnp.float32, -1.0, 1.0), -1.0, 1.0),
        "b_rec": jnp.clip(jax.random.uniform(streams_of[8], (3 * S,), jnp.float32, -1.0, 1.0), -1.0, 1.0),
    }


def gru_backward(carry_grad, inputs, states, w_in, w_rec, b_in, b_rec):
    width = states.shape[-1]
    from_input = jnp.dot(inputs, w_in, preferred_element_type=jnp.float32) + b_in
    from_state = jnp.dot(states, w_rec, preferred_element_type=jnp.float32) + b_rec
    update_gate = jax.nn.sigmoid(from_input[:, :width] + from_state[:, :width])
    reset_gate = jax.nn.sigmoid(from_input[:, width:2 * width] + from_state[:, width:2 * width])
    recur_part = from_state[:, 2 * width:]
    candidate = jnp.tanh(from_input[:, 2 * width:] + reset_gate * recur_part)
    state_wide = states.astype(jnp.float32)
    cand_pre = carry_grad * (1.0 - update_gate) * (1.0 - candidate * candidate)
    update_pre = carry_grad * (state_wide - candidate) * update_gate * (1.0 - update_gate)
    reset_pre = cand_pre * recur_part * reset_gate * (1.0 - reset_gate)
    input_pre = jnp.concatenate([update_pre, reset_pre, cand_pre], axis=1).astype(jnp.bfloat16)
    state_pre = jnp.concatenate([update_pre, reset_pre, cand_pre * reset_gate], axis=1).astype(jnp.bfloat16)
    input_grad = jnp.dot(input_pre, w_in.T, preferred_element_type=jnp.float32)
    state_grad = carry_grad * update_gate + jnp.dot(state_pre, w_rec.T, preferred_element_type=jnp.float32)
    w_in_term = jnp.dot(inputs.T, input_pre, preferred_element_type=jnp.float32)
    w_rec_term = jnp.dot(states.T, state_pre, preferred_element_type=jnp.float32)
    b_in_term = lax.optimization_barrier(jnp.sum(input_pre.astype(jnp.float32), axis=0))
    b_rec_term = lax.optimization_barrier(jnp.sum(state_pre.astype(jnp.float32), axis=0))
    return (state_grad, input_grad, w_in_term, w_rec_term, b_in_term, b_rec_term)

def reference(link_ids, path_states, final_grad, link_states, agg_grad, w_in, w_rec, b_in, b_rec):
    blocks = 64
    block_paths = PATHS // blocks
    width = link_states.shape[1]

    def one_block(carried, start):
        link_total, w_in_sum, w_rec_sum, b_in_sum, b_rec_sum = carried
        block_ids = lax.dynamic_slice_in_dim(link_ids, start, block_paths, 0)
        states = lax.dynamic_slice_in_dim(path_states, start, block_paths, 0)
        carry_grad = lax.dynamic_slice_in_dim(final_grad, start, block_paths, 0).astype(jnp.float32)
        for hop in range(HOPS - 1, -1, -1):
            column = block_ids[:, hop]
            carry_grad = carry_grad + agg_grad[column].astype(jnp.float32)
            carry_grad, input_grad, w_in_term, w_rec_term, b_in_term, b_rec_term = gru_backward(carry_grad, link_states[column], states[:, hop], w_in, w_rec, b_in, b_rec)
            link_total = link_total.at[column].add(input_grad)
            w_in_sum = w_in_sum + w_in_term
            w_rec_sum = w_rec_sum + w_rec_term
            b_in_sum = b_in_sum + b_in_term
            b_rec_sum = b_rec_sum + b_rec_term
        return ((link_total, w_in_sum, w_rec_sum, b_in_sum, b_rec_sum), carry_grad.astype(jnp.bfloat16))
    starts = (jnp.arange(blocks) * block_paths).astype(jnp.int32)
    zero_carry = (jnp.zeros((LINKS, width), jnp.float32), jnp.zeros((width, 3 * width), jnp.float32), jnp.zeros((width, 3 * width), jnp.float32), jnp.zeros((3 * width,), jnp.float32), jnp.zeros((3 * width,), jnp.float32))
    totals, path_grad = lax.scan(one_block, zero_carry, starts)
    path_grad = path_grad.reshape(PATHS, width)
    norm_scale = 1.0 / math.sqrt(PATHS * HOPS)
    return (path_grad, totals[0], totals[1] * norm_scale, totals[2] * norm_scale, totals[3] * norm_scale, totals[4] * norm_scale)
```

```python
import functools
import math

import jax
import jax.numpy as jnp
from jax import lax
from jax.experimental import pallas as pl
from jax.experimental.pallas import tpu as pltpu
from jax.sharding import PartitionSpec as P

MESH = pl.DeviceIdType.MESH
F32 = jnp.float32
BF16 = jnp.bfloat16
I32 = jnp.int32

OUTER = 32
GRP = 4
DEV = OUTER * GRP
HOPS = 8
PATHS = 768
LINKS = 768
WIDTH = 128
ROWS = PATHS * HOPS
CAP = 3 * ROWS // (2 * DEV)
STRIDE = 11
CHUNK = 256
NT = (((1,), (1,)), ((), ()))
TN = (((0,), (0,)), ((), ()))


def iota(shape, dim):
    return lax.broadcasted_iota(I32, shape, dim)


def kernel(
    ids_ref, states_ref, final_ref, link_ref, agg_ref, w_in_ref, w_rec_ref, b_in_ref, b_rec_ref,
    path_out, link_out, w_in_out, w_rec_out, bias_out,
    upper, owner_v, slot_v, asks, ask_send, ask_recv, ask_cols, pos_v, slot_s, pos_s, table,
    x_send, agg_send, x_recv, agg_recv, out_send, out_recv, rows_f, states_f, stage,
    coef_a, coef_b, coef_g, coef_r, coef_u, x_b, h_b, carry, w_part, w_recv, w_total, w_all, bias_acc,
    ask_ss, ask_rs, x_ss, x_rs, agg_ss, agg_rs, out_ss, out_rs, w1_ss, w1_rs, w2_ss, w2_rs, local_s,
):
    me_o = lax.axis_index("outer")
    me_g = lax.axis_index("grp")
    me = me_o * GRP + me_g

    def ahead(k):
        o = lax.rem(me_o + lax.rem((k // GRP) * STRIDE, OUTER), OUTER)
        g = lax.rem(me_g + lax.rem(k, GRP), GRP)
        return o, g, o * GRP + g

    def behind(k):
        o = lax.rem(me_o + OUTER - lax.rem((k // GRP) * STRIDE, OUTER), OUTER)
        g = lax.rem(me_g + GRP - lax.rem(k, GRP), GRP)
        return o * GRP + g

    def send(src, dst, send_sem, recv_sem, k):
        o, g, p = ahead(k)
        return pltpu.make_async_remote_copy(
            src_ref=src(p), dst_ref=dst, send_sem=send_sem.at[p], recv_sem=recv_sem.at[me],
            device_id=(o, g), device_id_type=MESH,
        )

    def arrived(dst, recv_sem, p):
        pltpu.make_async_copy(dst, dst, recv_sem.at[p]).wait()

    barrier = pltpu.get_barrier_semaphore()

    def greet(k, _):
        o, g, _p = ahead(k)
        pl.semaphore_signal(barrier, inc=1, device_id=(o, g), device_id_type=MESH)
        return 0

    lax.fori_loop(1, DEV, greet, 0)

    def upper_block(b, _):
        r = pl.multiple_of(b * 128, 128)
        upper[pl.ds(r, 128), :] = jnp.where(
            iota((128, PATHS), 0) + r < iota((128, PATHS), 1), 1.0, 0.0
        ).astype(BF16)
        return 0

    lax.fori_loop(0, PATHS // 128, upper_block, 0)
    owner_v[...] = ((ids_ref[...] >> 8) * 171) >> 9
    asks[...] = jnp.zeros_like(asks)

    def index_hop(t, base):
        own = owner_v[pl.ds(t, 1), :]
        local = ids_ref[pl.ds(t, 1), :] - own * LINKS + 1
        hot = iota((DEV, PATHS), 0) == own
        hot_b = jnp.where(hot, 1.0, 0.0).astype(BF16)
        before = jnp.dot(hot_b, upper[...], preferred_element_type=F32) + base
        rank = jnp.sum(jnp.where(hot, before, 0.0), axis=0, keepdims=True).astype(I32)
        slot_v[pl.ds(t, 1), :] = jnp.clip(own * CAP + rank, 0, DEV * CAP - 1)
        at_rank = iota((128, PATHS), 0) == rank
        pos = iota((1, PATHS), 1) + t * PATHS

        def parts(row, bits):
            high = (row >> bits).astype(F32)
            low = (row & ((1 << bits) - 1)).astype(F32)
            both = jnp.concatenate(
                [jnp.where(at_rank, high, 0.0), jnp.where(at_rank, low, 0.0)], axis=0
            ).astype(BF16)
            return lax.dot_general(hot_b, both, NT, preferred_element_type=F32)

        asks[:, :256] += parts(local, 5)
        asks[:, 256:] += parts(pos, 7)
        return base + jnp.sum(jnp.where(hot, 1.0, 0.0), axis=1, keepdims=True)

    lax.fori_loop(0, HOPS, index_hop, jnp.zeros((DEV, 1), F32))
    w_all[:DEV, :] = asks[:, :128] * 32.0 + asks[:, 128:256]
    pos_v[...] = jnp.clip((asks[:, 256:384] * 128.0 + asks[:, 384:]).astype(I32), 0, ROWS - 1)
    to_slots = pltpu.make_async_copy(slot_v, slot_s, local_s.at[0])
    to_pos = pltpu.make_async_copy(pos_v, pos_s, local_s.at[1])
    to_slots.start()
    to_pos.start()

    def spread(o, _):
        ask_send[o] = w_all[pl.ds(o, 1), :].astype(I32)
        return 0

    lax.fori_loop(0, DEV, spread, 0)
    ask_recv[me] = ask_send[me]
    pl.semaphore_wait(barrier, DEV - 1)

    def ask_copy(k):
        return send(lambda p: ask_send.at[p], ask_recv.at[me], ask_ss, ask_rs, k)

    def start_ask(k, _):
        ask_copy(k).start()
        return 0

    lax.fori_loop(1, DEV, start_ask, 0)

    table[:, :WIDTH] = link_ref[...]
    table[:, WIDTH:] = agg_ref[...]

    def widen(b, _):
        r = pl.multiple_of(b * 64, 64)
        block = states_ref[pl.ds(r, 64)].astype(F32)
        states_f[pl.ds(pl.multiple_of(b * 512, 512), 512), :] = block.reshape(512, WIDTH)
        return 0

    lax.fori_loop(0, PATHS // 64, widen, 0)
    carry[...] = final_ref[...].astype(F32)
    to_slots.wait()
    to_pos.wait()

    def wait_ask(k, _):
        p = behind(k)
        arrived(ask_recv.at[p], ask_rs, p)
        return 0

    lax.fori_loop(1, DEV, wait_ask, 0)
    ask_cols[...] = jnp.transpose((ask_recv[...].reshape(DEV, 128) - 1).astype(F32))

    def x_copy(k):
        return send(lambda p: x_send.at[p], x_recv.at[me], x_ss, x_rs, k)

    def agg_copy(k):
        return send(lambda p: agg_send.at[p], agg_recv.at[me], agg_ss, agg_rs, k)

    def answer(i, _):
        o = lax.rem(me_o + lax.rem(i * STRIDE, OUTER), OUTER)
        cols = []
        for g in range(GRP):
            mine = jnp.where(iota((CAP, 128), 1) == o * GRP + g, ask_cols[:CAP, :], 0.0)
            cols.append(jnp.sum(mine, axis=1, keepdims=True))
        col = jnp.concatenate(cols, axis=0).astype(I32)
        hot = jnp.where(iota((GRP * CAP, LINKS), 1) == col, 1.0, 0.0).astype(BF16)
        got = jnp.dot(hot, table[...], preferred_element_type=F32)
        for g in range(GRP):
            x_send[o * GRP + g] = got[g * CAP : (g + 1) * CAP, :WIDTH].astype(BF16)
            agg_send[o * GRP + g] = got[g * CAP : (g + 1) * CAP, WIDTH:].astype(BF16)
        for g in range(GRP):
            if g == 0:
                @pl.when(i > 0)
                def _():
                    x_copy(i * GRP).start()
            else:
                x_copy(i * GRP + g).start()
        return 0

    lax.fori_loop(0, OUTER, answer, 0)

    def start_agg(k, _):
        agg_copy(k).start()
        return 0

    lax.fori_loop(1, DEV, start_agg, 0)
    x_recv[me] = x_send[me]
    agg_recv[me] = agg_send[me]

    def take(recv, recv_sem):
        def body(k, _):
            p = behind(k)

            @pl.when(k > 0)
            def _():
                arrived(recv.at[p], recv_sem, p)

            rows_f[pl.ds(pl.multiple_of(p * CAP, 8), CAP), :] = recv[p].astype(F32)
            return 0

        lax.fori_loop(0, DEV, body, 0)

    def to_path_order(t):
        def body(b, _):
            r = pl.multiple_of(b * 16, 16)
            for j in range(16):
                stage[pl.ds(r + j, 1), :] = rows_f[pl.ds(slot_s[t, r + j], 1), :]
            return 0

        lax.fori_loop(0, PATHS // 16, body, 0)

    take(x_recv, x_rs)

    def forward_hop(t, _):
        to_path_order(t)

        def chunk(c, _):
            r = pl.multiple_of(c * CHUNK, CHUNK)
            out = pl.ds(pl.multiple_of(t * PATHS + r, CHUNK), CHUNK)
            x = stage[pl.ds(r, CHUNK), :].astype(BF16)
            h = states_f[pl.ds(r * HOPS + t, CHUNK, stride=HOPS), :]
            hb = h.astype(BF16)
            x_b[out, :] = x
            h_b[out, :] = hb
            gx = jnp.dot(x, w_in_ref[...], preferred_element_type=F32) + b_in_ref[...]
            gh = jnp.dot(hb, w_rec_ref[...], preferred_element_type=F32) + b_rec_ref[...]
            u = jax.nn.sigmoid(gx[:, :WIDTH] + gh[:, :WIDTH])
            r_gate = jax.nn.sigmoid(gx[:, WIDTH : 2 * WIDTH] + gh[:, WIDTH : 2 * WIDTH])
            recur = gh[:, 2 * WIDTH :]
            cand = jnp.tanh(gx[:, 2 * WIDTH :] + r_gate * recur)
            coef_a[out, :] = (1.0 - u) * (1.0 - cand * cand)
            coef_b[out, :] = (h - cand) * u * (1.0 - u)
            coef_g[out, :] = recur * r_gate * (1.0 - r_gate)
            coef_r[out, :] = r_gate
            coef_u[out, :] = u
            return 0

        lax.fori_loop(0, PATHS // CHUNK, chunk, 0)
        return 0

    lax.fori_loop(0, HOPS, forward_hop, 0)
    take(agg_recv, agg_rs)
    w_in_out[...] = jnp.zeros_like(w_in_out)
    w_rec_out[...] = jnp.zeros_like(w_rec_out)
    bias_acc[...] = jnp.zeros_like(bias_acc)
    grads = coef_a

    def backward_hop(i, _):
        t = HOPS - 1 - i
        to_path_order(t)

        def chunk(c, _):
            r = pl.multiple_of(c * CHUNK, CHUNK)
            here = pl.ds(r, CHUNK)
            out = pl.ds(pl.multiple_of(t * PATHS + r, CHUNK), CHUNK)
            cg = carry[here, :] + stage[here, :]
            pc = cg * coef_a[out, :]
            pu = (cg * coef_b[out, :]).astype(BF16)
            pr = (pc * coef_g[out, :]).astype(BF16)
            pcr = (pc * coef_r[out, :]).astype(BF16)
            in_pre = jnp.concatenate([pu, pr, pc.astype(BF16)], axis=1)
            st_pre = jnp.concatenate([pu, pr, pcr], axis=1)
            carry[here, :] = cg * coef_u[out, :] + lax.dot_general(
                st_pre, w_rec_ref[...], NT, preferred_element_type=F32
            )
            grads[out, :] = lax.dot_general(in_pre, w_in_ref[...], NT, preferred_element_type=F32)
            w_in_out[...] += lax.dot_general(x_b[out, :], in_pre, TN, preferred_element_type=F32)
            w_rec_out[...] += lax.dot_general(h_b[out, :], st_pre, TN, preferred_element_type=F32)
            bias_acc[0:1, :] += jnp.sum(in_pre.astype(F32), axis=0, keepdims=True)
            bias_acc[1:2, :] += jnp.sum(st_pre.astype(F32), axis=0, keepdims=True)
            return 0

        lax.fori_loop(0, PATHS // CHUNK, chunk, 0)
        return 0

    lax.fori_loop(0, HOPS, backward_hop, 0)
    path_out[...] = carry[...].astype(BF16)

    for r in range(3):
        lanes = slice(r * WIDTH, (r + 1) * WIDTH)
        w_part[pl.ds(r, DEV, stride=8), :] = w_in_out[:, lanes]
        w_part[pl.ds(3 + r, DEV, stride=8), :] = w_rec_out[:, lanes]
    bias8 = jnp.concatenate(
        [bias_acc[0:1, r * WIDTH : (r + 1) * WIDTH] for r in range(3)]
        + [bias_acc[1:2, r * WIDTH : (r + 1) * WIDTH] for r in range(3)]
        + [jnp.zeros((2, WIDTH), F32)],
        axis=0,
    )
    w_part[pl.ds(6, DEV, stride=8), :] = jnp.concatenate([bias8] * (DEV // 8), axis=0)
    w_part[pl.ds(7, DEV, stride=8), :] = jnp.zeros((DEV, WIDTH), F32)

    def rows8(ref, p):
        return ref.at[pl.ds(pl.multiple_of(p * 8, 8), 8), :]

    def part_copy(k):
        return send(lambda p: rows8(w_part, p), rows8(w_recv, me), w1_ss, w1_rs, k)

    def start_part(k, _):
        part_copy(k).start()
        return 0

    lax.fori_loop(1, DEV, start_part, 0)

    def out_copy(k):
        return send(lambda p: out_send.at[p], out_recv.at[me], out_ss, out_rs, k)

    def give(k, _):
        _o, _g, p = ahead(k)
        for j in range(CAP):
            stage[pl.ds(j, 1), :] = grads[pl.ds(pos_s[p, j], 1), :]
        out_send[p] = stage[:CAP, :].astype(BF16)

        @pl.when(k > 0)
        def _():
            out_copy(k).start()

        return 0

    lax.fori_loop(0, DEV, give, 0)
    out_recv[me] = out_send[me]

    own_rows = pl.ds(pl.multiple_of(me * 8, 8), 8)

    def add_part(k, total):
        p = behind(k)
        arrived(rows8(w_recv, p), w1_rs, p)
        return total + w_recv[pl.ds(pl.multiple_of(p * 8, 8), 8), :]

    total = lax.fori_loop(1, DEV, add_part, w_part[own_rows, :]) * (1.0 / math.sqrt(ROWS * DEV))
    w_total[...] = total

    def total_copy(k):
        return send(lambda p: w_total, rows8(w_all, me), w2_ss, w2_rs, k)

    def start_total(k, _):
        total_copy(k).start()
        return 0

    lax.fori_loop(1, DEV, start_total, 0)
    w_all[own_rows, :] = total

    link_out[...] = jnp.zeros_like(link_out)

    def collect(k, _):
        p = behind(k)

        @pl.when(k > 0)
        def _():
            arrived(out_recv.at[p], out_rs, p)

        hot = jnp.where(iota((LINKS, 128), 0) == ask_recv[p] - 1, 1.0, 0.0).astype(BF16)
        link_out[...] += jnp.dot(hot[:, :CAP], out_recv[p], preferred_element_type=F32)
        return 0

    lax.fori_loop(0, DEV, collect, 0)

    def wait_total(k, _):
        p = behind(k)
        arrived(rows8(w_all, p), w2_rs, p)
        return 0

    lax.fori_loop(1, DEV, wait_total, 0)
    for r in range(3):
        lanes = slice(r * WIDTH, (r + 1) * WIDTH)
        w_in_out[:, lanes] = w_all[pl.ds(r, DEV, stride=8), :]
        w_rec_out[:, lanes] = w_all[pl.ds(3 + r, DEV, stride=8), :]
    bias_out[...] = w_all[pl.ds(6, 8, stride=8), :]

    def sent(k, _):
        for copy in (ask_copy(k), x_copy(k), agg_copy(k), part_copy(k), out_copy(k), total_copy(k)):
            copy.wait_send()
        return 0

    lax.fori_loop(1, DEV, sent, 0)


def per_device(link_ids, path_states, final_grad, link_states, agg_grad, w_in, w_rec, b_in, b_rec):
    vmem = pl.BlockSpec(memory_space=pltpu.VMEM)
    dma = pltpu.SemaphoreType.DMA((DEV,))
    rows_pair = pltpu.VMEM((DEV, CAP, WIDTH), BF16)
    wide = pltpu.VMEM((ROWS, WIDTH), F32)
    path_grad, link_grad, w_in_grad, w_rec_grad, bias = pl.pallas_call(
        kernel,
        out_shape=(
            jax.ShapeDtypeStruct((PATHS, WIDTH), BF16),
            jax.ShapeDtypeStruct((LINKS, WIDTH), F32),
            jax.ShapeDtypeStruct((WIDTH, 3 * WIDTH), F32),
            jax.ShapeDtypeStruct((WIDTH, 3 * WIDTH), F32),
            jax.ShapeDtypeStruct((8, WIDTH), F32),
        ),
        in_specs=[vmem] * 9,
        out_specs=(vmem,) * 5,
        scratch_shapes=[
            pltpu.VMEM((PATHS, PATHS), BF16),
            pltpu.VMEM((HOPS, PATHS), I32),
            pltpu.VMEM((HOPS, PATHS), I32),
            pltpu.VMEM((DEV, 512), F32),
            pltpu.VMEM((DEV, 1, 128), I32),
            pltpu.VMEM((DEV, 1, 128), I32),
            pltpu.VMEM((128, DEV), F32),
            pltpu.VMEM((DEV, 128), I32),
            pltpu.SMEM((HOPS, PATHS), I32),
            pltpu.SMEM((DEV, 128), I32),
            pltpu.VMEM((LINKS, 2 * WIDTH), BF16),
            rows_pair, rows_pair, rows_pair, rows_pair, rows_pair, rows_pair,
            pltpu.VMEM((DEV * CAP, WIDTH), F32),
            pltpu.VMEM((ROWS + 8, WIDTH), F32),
            pltpu.VMEM((PATHS, WIDTH), F32),
            wide, wide, wide, wide, wide,
            pltpu.VMEM((ROWS, WIDTH), BF16),
            pltpu.VMEM((ROWS, WIDTH), BF16),
            pltpu.VMEM((PATHS, WIDTH), F32),
            pltpu.VMEM((DEV * 8 + 8, WIDTH), F32),
            pltpu.VMEM((DEV * 8 + 8, WIDTH), F32),
            pltpu.VMEM((8, WIDTH), F32),
            pltpu.VMEM((DEV * 8 + 8, WIDTH), F32),
            pltpu.VMEM((8, 3 * WIDTH), F32),
        ] + [dma] * 12 + [pltpu.SemaphoreType.DMA((2,))],
        compiler_params=pltpu.CompilerParams(
            collective_id=0, has_side_effects=True, vmem_limit_bytes=60 * 2**20
        ),
    )(
        jnp.transpose(link_ids), path_states, final_grad, link_states, agg_grad, w_in, w_rec,
        b_in.reshape(1, 3 * WIDTH), b_rec.reshape(1, 3 * WIDTH),
    )
    return (
        path_grad, link_grad, w_in_grad, w_rec_grad,
        bias[:3].reshape(3 * WIDTH), bias[3:6].reshape(3 * WIDTH),
    )


def solution(mesh):
    rows = P(("outer", "grp"), None)
    return jax.shard_map(
        per_device,
        mesh=mesh,
        in_specs=(rows, P(("outer", "grp"), None, None), rows, rows, rows, P(), P(), P(), P()),
        out_specs=(rows, rows, P(), P(), P(), P()),
        check_vma=False,
    )
```

```python
import functools
import math

import jax
import jax.numpy as jnp
from jax import lax
from jax.experimental import pallas as pl
from jax.experimental.pallas import tpu as pltpu
from jax.sharding import PartitionSpec as P

MESH = pl.DeviceIdType.MESH
F32 = jnp.float32
BF16 = jnp.bfloat16
I32 = jnp.int32

OUTER = 32
GRP = 4
DEV = OUTER * GRP
HOPS = 8
PATHS = 768
LINKS = 768
WIDTH = 128
ROWS = PATHS * HOPS
CAP = 3 * ROWS // (2 * DEV)
STRIDE = 11
CHUNK = 256
NT = (((1,), (1,)), ((), ()))
TN = (((0,), (0,)), ((), ()))


def iota(shape, dim):
    return lax.broadcasted_iota(I32, shape, dim)


def kernel(
    ids_ref, states_ref, final_ref, link_ref, agg_ref, w_in_ref, w_rec_ref, b_in_ref, b_rec_ref,
    path_out, link_out, w_in_out, w_rec_out, bias_out,
    upper, owner_v, slot_v, asks, ask_rows, pos_rows, ask_send, ask_recv, ask_cols, pos_v, slot_s, pos_s, table,
    x_send, agg_send, x_recv, agg_recv, out_send, out_recv, rows_f, states_f, stage,
    coef_a, coef_b, coef_g, coef_r, coef_u, xh, pre, carry, w_big, w_sum, w_part, w_pair, w_recv, w_total, w_all,
    ask_ss, ask_rs, x_ss, x_rs, agg_ss, agg_rs, out_ss, out_rs, w1_ss, w1_rs, w2_ss, w2_rs, pair_s, local_s,
):
    me_o = lax.axis_index("outer")
    me_g = lax.axis_index("grp")
    me = me_o * GRP + me_g

    grps = [lax.rem(me_g + q, GRP) for q in range(GRP)]

    def ahead(i):
        return lax.rem(me_o + lax.rem(i * STRIDE, OUTER), OUTER)

    def behind(i):
        return lax.rem(me_o + OUTER - lax.rem(i * STRIDE, OUTER), OUTER)

    def to_others(act):
        for q in range(1, GRP):
            act(me_o, grps[q])

        def body(i, _):
            o = ahead(i)
            for q in range(GRP):
                act(o, grps[q])
            return 0

        lax.fori_loop(1, OUTER, body, 0)

    def send(src, dst, send_sem, recv_sem, o, g):
        pltpu.make_async_remote_copy(
            src_ref=src, dst_ref=dst, send_sem=send_sem, recv_sem=recv_sem,
            device_id=(o, g), device_id_type=MESH,
        ).start()

    def done(ref, sem):
        pltpu.make_async_copy(ref, ref, sem).wait()

    barrier = pltpu.get_barrier_semaphore()
    to_others(
        lambda o, g: pl.semaphore_signal(barrier, inc=1, device_id=(o, g), device_id_type=MESH)
    )

    def upper_block(b, _):
        r = pl.multiple_of(b * 128, 128)
        upper[pl.ds(r, 128), :] = jnp.where(
            iota((128, PATHS), 0) + r < iota((128, PATHS), 1), 1.0, 0.0
        ).astype(BF16)
        return 0

    lax.fori_loop(0, PATHS // 128, upper_block, 0)
    owner_v[...] = ((ids_ref[...] >> 8) * 171) >> 9
    asks[...] = jnp.zeros_like(asks)

    def index_hop(t, base):
        own = owner_v[pl.ds(t, 1), :]
        local = ids_ref[pl.ds(t, 1), :] - own * LINKS + 1
        hot = iota((DEV, PATHS), 0) == own
        hot_b = jnp.where(hot, 1.0, 0.0).astype(BF16)
        before = jnp.dot(hot_b, upper[...], preferred_element_type=F32) + base
        rank = jnp.sum(jnp.where(hot, before, 0.0), axis=0, keepdims=True).astype(I32)
        slot = jnp.clip(own * CAP + rank, 0, DEV * CAP - 1)
        slot_v[pl.ds(pl.multiple_of(t * PATHS, PATHS), PATHS)] = slot.reshape(PATHS)
        at_rank = iota((128, PATHS), 0) == rank
        pos = iota((1, PATHS), 1) + t * PATHS

        def parts(row, bits):
            high = (row >> bits).astype(F32)
            low = (row & ((1 << bits) - 1)).astype(F32)
            both = jnp.concatenate(
                [jnp.where(at_rank, high, 0.0), jnp.where(at_rank, low, 0.0)], axis=0
            ).astype(BF16)
            return lax.dot_general(hot_b, both, NT, preferred_element_type=F32)

        asks[:, :256] += parts(local, 5)
        asks[:, 256:] += parts(pos, 7)
        return base + jnp.sum(jnp.where(hot, 1.0, 0.0), axis=1, keepdims=True)

    lax.fori_loop(0, HOPS, index_hop, jnp.zeros((DEV, 1), F32))
    ask_rows[...] = (asks[:, :128] * 32.0 + asks[:, 128:256]).astype(I32)
    pos = (asks[:, 256:384] * 128.0 + asks[:, 384:]).astype(I32)
    pos_rows[...] = jnp.clip(pos, 0, ROWS - 1)

    def spread(o, _):
        ask_send[o] = ask_rows[pl.ds(o, 1), :]
        pos = pos_rows[pl.ds(o, 1), :]
        pos_v[pl.ds(pl.multiple_of(o * 128, 128), 128)] = pos.reshape(128)
        return 0

    lax.fori_loop(0, DEV, spread, 0)
    to_slots = pltpu.make_async_copy(slot_v, slot_s, local_s.at[0])
    to_pos = pltpu.make_async_copy(pos_v, pos_s, local_s.at[1])
    to_slots.start()
    to_pos.start()

    ask_recv[me] = ask_send[me]
    pl.semaphore_wait(barrier, DEV - 1)

    to_others(
        lambda o, g: send(ask_send.at[o * GRP + g], ask_recv.at[me], ask_ss, ask_rs, o, g)
    )

    table[:, :WIDTH] = link_ref[...]
    table[:, WIDTH:] = agg_ref[...]

    def widen(b, _):
        r = pl.multiple_of(b * 64, 64)
        block = states_ref[pl.ds(r, 64)].astype(F32)
        states_f[pl.ds(pl.multiple_of(b * 512, 512), 512), :] = block.reshape(512, WIDTH)
        return 0

    lax.fori_loop(0, PATHS // 64, widen, 0)
    carry[...] = final_ref[...].astype(F32)
    third = 2 * WIDTH
    none = jnp.zeros((WIDTH, WIDTH), BF16)
    w_big[:WIDTH, : 3 * WIDTH] = w_in_ref[...]
    w_big[:WIDTH, 3 * WIDTH :] = none
    w_big[WIDTH:, :third] = w_rec_ref[:, :third]
    w_big[WIDTH:, third : 3 * WIDTH] = none
    w_big[WIDTH:, 3 * WIDTH :] = w_rec_ref[:, third:]
    b_in = b_in_ref[...].reshape(1, 3 * WIDTH)
    b_rec = b_rec_ref[...].reshape(1, 3 * WIDTH)
    bias = jnp.concatenate(
        [b_in[:, :third] + b_rec[:, :third], b_in[:, third:], b_rec[:, third:]], axis=1
    )
    to_slots.wait()
    to_pos.wait()

    done(ask_recv.at[pl.ds(0, DEV - 1)], ask_rs)
    ask_cols[...] = jnp.transpose((ask_recv[...].reshape(DEV, 128) - 1).astype(F32))

    def answer(i, first):
        o = ahead(i)
        cols = []
        for g in range(GRP):
            mine = jnp.where(iota((CAP, 128), 1) == o * GRP + g, ask_cols[:CAP, :], 0.0)
            cols.append(jnp.sum(mine, axis=1, keepdims=True))
        col = jnp.concatenate(cols, axis=0).astype(I32)
        hot = jnp.where(iota((GRP * CAP, LINKS), 1) == col, 1.0, 0.0).astype(BF16)
        got = jnp.dot(hot, table[...], preferred_element_type=F32)
        for g in range(GRP):
            x_send[o * GRP + g] = got[g * CAP : (g + 1) * CAP, :WIDTH].astype(BF16)
            agg_send[o * GRP + g] = got[g * CAP : (g + 1) * CAP, WIDTH:].astype(BF16)
        for q in range(first, GRP):
            p = o * GRP + grps[q]
            send(x_send.at[p], x_recv.at[me], x_ss, x_rs.at[me_o], o, grps[q])
        return 0

    answer(0, 1)
    lax.fori_loop(1, OUTER, lambda i, _: answer(i, 0), 0)
    x_recv[me] = x_send[me]
    agg_recv[me] = agg_send[me]

    def send_agg(o, first):
        for q in range(first, GRP):
            p = o * GRP + grps[q]
            send(agg_send.at[p], agg_recv.at[me], agg_ss, agg_rs.at[me_o], o, grps[q])

    def take(recv, recv_sem, then):
        def rows_of(o):
            block = recv[pl.ds(o * GRP, GRP)].astype(F32).reshape(GRP * CAP, WIDTH)
            rows_f[pl.ds(pl.multiple_of(o * GRP * CAP, 8), GRP * CAP), :] = block

        done(recv.at[pl.ds(0, GRP - 1)], recv_sem.at[me_o])
        rows_of(me_o)
        then(me_o, 1)

        def body(i, _):
            o = behind(i)
            done(recv.at[pl.ds(o * GRP, GRP)], recv_sem.at[o])
            then(ahead(i), 0)
            rows_of(o)
            return 0

        lax.fori_loop(1, OUTER, body, 0)

    def to_path_order(t):
        def body(b, _):
            r = pl.multiple_of(b * 32, 32)
            got = [rows_f[pl.ds(slot_s[t * PATHS + r + j], 1), :] for j in range(32)]
            for j in range(32):
                stage[pl.ds(r + j, 1), :] = got[j]
            return 0

        lax.fori_loop(0, PATHS // 32, body, 0)

    take(x_recv, x_rs, send_agg)

    def forward_hop(t, _):
        to_path_order(t)

        def chunk(c, _):
            r = pl.multiple_of(c * CHUNK, CHUNK)
            out = pl.ds(pl.multiple_of(t * PATHS + r, CHUNK), CHUNK)
            h = states_f[pl.ds(r * HOPS + t, CHUNK, stride=HOPS), :]
            xh[out, :WIDTH] = stage[pl.ds(r, CHUNK), :].astype(BF16)
            xh[out, WIDTH:] = h.astype(BF16)
            both = jnp.dot(xh[out, :], w_big[...], preferred_element_type=F32) + bias
            u = jax.nn.sigmoid(both[:, :WIDTH])
            r_gate = jax.nn.sigmoid(both[:, WIDTH : 2 * WIDTH])
            recur = both[:, 3 * WIDTH :]
            cand = jnp.tanh(both[:, 2 * WIDTH : 3 * WIDTH] + r_gate * recur)
            coef_a[out, :] = (1.0 - u) * (1.0 - cand * cand)
            coef_b[out, :] = (h - cand) * u * (1.0 - u)
            coef_g[out, :] = recur * r_gate * (1.0 - r_gate)
            coef_r[out, :] = r_gate
            coef_u[out, :] = u
            return 0

        lax.fori_loop(0, PATHS // CHUNK, chunk, 0)
        return 0

    lax.fori_loop(0, HOPS, forward_hop, 0)
    take(agg_recv, agg_rs, lambda o, first: None)
    grads = coef_a

    def backward_hop(i, _):
        t = HOPS - 1 - i
        to_path_order(t)

        def chunk(c, _):
            r = pl.multiple_of(c * CHUNK, CHUNK)
            here = pl.ds(r, CHUNK)
            out = pl.ds(pl.multiple_of(t * PATHS + r, CHUNK), CHUNK)
            cg = carry[here, :] + stage[here, :]
            pc = cg * coef_a[out, :]
            parts = [cg * coef_b[out, :], pc * coef_g[out, :], pc, pc * coef_r[out, :]]
            rounded = jnp.concatenate([part.astype(BF16) for part in parts], axis=1)
            pre[out, :] = rounded
            back = lax.dot_general(rounded, w_big[...], NT, preferred_element_type=F32)
            grads[out, :] = back[:, :WIDTH]
            carry[here, :] = cg * coef_u[out, :] + back[:, WIDTH:]
            return 0

        lax.fori_loop(0, PATHS // CHUNK, chunk, 0)
        return 0

    lax.fori_loop(0, HOPS, backward_hop, 0)

    def give(o, g):
        p = o * GRP + g
        for first in range(0, CAP, 24):
            got = [grads[pl.ds(pos_s[p * 128 + first + j], 1), :] for j in range(24)]
            for j in range(24):
                stage[pl.ds(first + j, 1), :] = got[j]
        out_send[p] = stage[:CAP, :].astype(BF16)

    def give_group(i, _):
        o = ahead(i)
        for q in range(GRP):
            give(o, grps[q])
            send(out_send.at[o * GRP + grps[q]], out_recv.at[me], out_ss, out_rs.at[me_o], o, grps[q])
        return 0

    def rows8(ref, n):
        return ref.at[pl.ds(pl.multiple_of(n * 8, 8), 8), :]

    core = lax.rem(me_o, 2)
    chip = me_o // 2
    seat = chip * GRP + me_g
    half = DEV // 2
    mine = pl.ds(pl.multiple_of(core * half * 8, 8), half * 8)
    theirs = pl.ds(pl.multiple_of((1 - core) * half * 8, 8), half * 8)
    twin = me_o + 1 - 2 * core

    def to_same_core(act):
        for q in range(1, GRP):
            act(chip, grps[q])

        def body(i, _):
            z = lax.rem(chip + lax.rem(i * 5, OUTER // 2), OUTER // 2)
            for q in range(GRP):
                act(z, grps[q])
            return 0

        lax.fori_loop(1, OUTER // 2, body, 0)

    lax.fori_loop(1, 6, give_group, 0)
    w_sum[...] = jnp.zeros_like(w_sum)

    def weights(c, sums):
        rows = pl.ds(pl.multiple_of(c * PATHS, PATHS), PATHS)
        w_sum[...] += lax.dot_general(xh[rows, :], pre[rows, :], TN, preferred_element_type=F32)
        return sums + jnp.sum(pre[rows, :].astype(F32), axis=0, keepdims=True)

    sums = lax.fori_loop(0, HOPS, weights, jnp.zeros((1, 4 * WIDTH), F32))

    w_rows = [w_sum[:WIDTH, r * WIDTH : (r + 1) * WIDTH] for r in (0, 1, 2)]
    w_rows += [w_sum[WIDTH:, r * WIDTH : (r + 1) * WIDTH] for r in (0, 1, 3)]
    for r in range(6):
        w_part[pl.ds(r, DEV, stride=8), :] = w_rows[r]
    bias8 = jnp.concatenate(
        [sums[:, r * WIDTH : (r + 1) * WIDTH] for r in (0, 1, 2, 0, 1, 3)]
        + [jnp.zeros((2, WIDTH), F32)],
        axis=0,
    )
    w_part[pl.ds(6, DEV, stride=8), :] = jnp.concatenate([bias8] * (DEV // 8), axis=0)
    w_part[pl.ds(7, DEV, stride=8), :] = jnp.zeros((DEV, WIDTH), F32)
    send(w_part.at[theirs, :], w_pair, pair_s.at[0], pair_s.at[1], twin, me_g)
    lax.fori_loop(6, 14, give_group, 0)
    done(w_pair, pair_s.at[1])
    w_pair[...] += w_part[mine, :]
    to_same_core(
        lambda z, g: send(
            rows8(w_pair, z * GRP + g), rows8(w_recv, seat), w1_ss, w1_rs, z * 2 + core, g
        )
    )
    lax.fori_loop(14, 26, give_group, 0)
    done(w_recv.at[pl.ds(0, (half - 1) * 8)], w1_rs)
    own_rows = pl.ds(pl.multiple_of(seat * 8, 8), 8)
    w_recv[own_rows, :] = w_pair[own_rows, :]
    total = jnp.sum(w_recv[...].reshape(half, 8, WIDTH), axis=0)
    total = total * (1.0 / math.sqrt(ROWS * DEV))
    w_total[...] = total
    line = core * half + seat
    to_same_core(
        lambda z, g: send(w_total, rows8(w_all, line), w2_ss, w2_rs, z * 2 + core, g)
    )
    w_all[pl.ds(pl.multiple_of(line * 8, 8), 8), :] = total
    lax.fori_loop(26, OUTER, give_group, 0)
    for q in range(1, GRP):
        give(me_o, grps[q])
        send(out_send.at[me_o * GRP + grps[q]], out_recv.at[me], out_ss, out_rs.at[me_o], me_o, grps[q])
    give(me_o, me_g)
    out_recv[me] = out_send[me]
    path_out[...] = carry[...].astype(BF16)

    link_out[...] = jnp.zeros_like(link_out)

    def collect(o):
        part = jnp.zeros((LINKS, WIDTH), F32)
        for g in range(GRP):
            p = o * GRP + g
            hot = jnp.where(iota((LINKS, 128), 0) == ask_recv[p] - 1, 1.0, 0.0).astype(BF16)
            part += jnp.dot(hot[:, :CAP], out_recv[p], preferred_element_type=F32)
        link_out[...] += part

    def collect_next(i, _):
        o = behind(i)
        done(out_recv.at[pl.ds(o * GRP, GRP)], out_rs.at[o])
        collect(o)
        return 0

    lax.fori_loop(1, OUTER // 2, collect_next, 0)
    done(w_all.at[pl.ds(0, (half - 1) * 8)], w2_rs)
    send(w_all.at[mine, :], w_all.at[mine, :], pair_s.at[2], pair_s.at[3], twin, me_g)
    lax.fori_loop(OUTER // 2, OUTER, collect_next, 0)
    done(out_recv.at[pl.ds(0, GRP - 1)], out_rs.at[me_o])
    collect(me_o)
    done(w_all.at[theirs, :], pair_s.at[3])
    for r in range(3):
        lanes = slice(r * WIDTH, (r + 1) * WIDTH)
        w_in_out[:, lanes] = w_all[pl.ds(r, DEV, stride=8), :]
        w_rec_out[:, lanes] = w_all[pl.ds(3 + r, DEV, stride=8), :]
    bias_out[...] = w_all[pl.ds(6, 8, stride=8), :]

    for buf, sem in (
        (ask_send, ask_ss), (x_send, x_ss), (agg_send, agg_ss), (out_send, out_ss)
    ):
        done(buf.at[pl.ds(0, DEV - 1)], sem)
    done(w_recv.at[pl.ds(0, (half - 1) * 8)], w1_ss)
    done(w_recv.at[pl.ds(0, (half - 1) * 8)], w2_ss)
    done(w_pair, pair_s.at[0])
    done(w_pair, pair_s.at[2])


def finish(path, link, w_in, w_rec, bias, path_out, link_out, w_in_out, w_rec_out, b_in_out, b_rec_out):
    path_out[...] = path[...]
    link_out[...] = link[...]
    w_in_out[...] = w_in[...]
    w_rec_out[...] = w_rec[...]
    for r in range(3):
        b_in_out[pl.ds(r * WIDTH, WIDTH)] = bias[r, :]
        b_rec_out[pl.ds(r * WIDTH, WIDTH)] = bias[3 + r, :]


def per_device(link_ids, path_states, final_grad, link_states, agg_grad, w_in, w_rec, b_in, b_rec):
    vmem = pl.BlockSpec(memory_space=pltpu.VMEM)
    one = pltpu.SemaphoreType.DMA
    some = pltpu.SemaphoreType.DMA((OUTER,))
    rows_pair = pltpu.VMEM((DEV, CAP, WIDTH), BF16)
    wide = pltpu.VMEM((ROWS, WIDTH), F32)
    shapes = (
        jax.ShapeDtypeStruct((PATHS, WIDTH), BF16),
        jax.ShapeDtypeStruct((LINKS, WIDTH), F32),
        jax.ShapeDtypeStruct((WIDTH, 3 * WIDTH), F32),
        jax.ShapeDtypeStruct((WIDTH, 3 * WIDTH), F32),
    )
    results = pl.pallas_call(
        kernel,
        out_shape=shapes + (jax.ShapeDtypeStruct((8, WIDTH), F32),),
        in_specs=[vmem] * 9,
        out_specs=(vmem,) * 5,
        scratch_shapes=[
            pltpu.VMEM((PATHS, PATHS), BF16),
            pltpu.VMEM((HOPS, PATHS), I32),
            pltpu.VMEM((ROWS,), I32),
            pltpu.VMEM((DEV, 512), F32),
            pltpu.VMEM((DEV, 128), I32),
            pltpu.VMEM((DEV, 128), I32),
            pltpu.VMEM((DEV, 1, 128), I32),
            pltpu.VMEM((DEV, 1, 128), I32),
            pltpu.VMEM((128, DEV), F32),
            pltpu.VMEM((DEV * 128,), I32),
            pltpu.SMEM((ROWS,), I32),
            pltpu.SMEM((DEV * 128,), I32),
            pltpu.VMEM((LINKS, 2 * WIDTH), BF16),
            rows_pair, rows_pair, rows_pair, rows_pair, rows_pair, rows_pair,
            pltpu.VMEM((DEV * CAP, WIDTH), F32),
            pltpu.VMEM((ROWS + 8, WIDTH), F32),
            pltpu.VMEM((PATHS, WIDTH), F32),
            wide, wide, wide, wide, wide,
            pltpu.VMEM((ROWS, 2 * WIDTH), BF16),
            pltpu.VMEM((ROWS, 4 * WIDTH), BF16),
            pltpu.VMEM((PATHS, WIDTH), F32),
            pltpu.VMEM((2 * WIDTH, 4 * WIDTH), BF16),
            pltpu.VMEM((2 * WIDTH, 4 * WIDTH), F32),
            pltpu.VMEM((DEV * 8 + 8, WIDTH), F32),
            pltpu.VMEM((DEV * 4, WIDTH), F32),
            pltpu.VMEM((DEV * 4, WIDTH), F32),
            pltpu.VMEM((8, WIDTH), F32),
            pltpu.VMEM((DEV * 8 + 8, WIDTH), F32),
        ] + [one, one, one, some, one, some, one, some, one, one, one, one]
        + [pltpu.SemaphoreType.DMA((4,)), pltpu.SemaphoreType.DMA((2,))],
        compiler_params=pltpu.CompilerParams(
            collective_id=0, has_side_effects=True, vmem_limit_bytes=60 * 2**20
        ),
    )(
        jnp.transpose(link_ids), path_states, final_grad, link_states, agg_grad, w_in, w_rec,
        b_in, b_rec,
    )
    flat = jax.ShapeDtypeStruct((3 * WIDTH,), F32)
    return pl.pallas_call(
        finish,
        out_shape=shapes + (flat, flat),
        in_specs=[vmem] * 5,
        out_specs=(vmem,) * 6,
    )(*results)


def solution(mesh):
    rows = P(("outer", "grp"), None)
    return jax.shard_map(
        per_device,
        mesh=mesh,
        in_specs=(rows, P(("outer", "grp"), None, None), rows, rows, rows, P(), P(), P(), P()),
        out_specs=(rows, rows, P(), P(), P(), P()),
        check_vma=False,
    )
```

```python
import functools
import math

import jax
import jax.numpy as jnp
from jax import lax
from jax.experimental import pallas as pl
from jax.experimental.pallas import tpu as pltpu
from jax.sharding import PartitionSpec as P

MESH = pl.DeviceIdType.MESH
F32 = jnp.float32
BF16 = jnp.bfloat16
I32 = jnp.int32

OUTER = 32
GRP = 4
DEV = OUTER * GRP
HOPS = 8
PATHS = 768
LINKS = 768
WIDTH = 128
ROWS = PATHS * HOPS
CAP = 3 * ROWS // (2 * DEV)
STRIDE = 11
CHUNK = 768
NT = (((1,), (1,)), ((), ()))
TN = (((0,), (0,)), ((), ()))


def iota(shape, dim):
    return lax.broadcasted_iota(I32, shape, dim)


def kernel(
    ids_ref, states_ref, final_ref, link_ref, agg_ref, w_in_ref, w_rec_ref, b_in_ref, b_rec_ref,
    path_out, link_out, w_in_out, w_rec_out, bias_out,
    upper, owner_v, slot_v, asks, ask_rows, pos_rows, ask_send, ask_recv, ask_cols, pos_v, slot_s, pos_s, table,
    x_send, agg_send, x_recv, agg_recv, out_send, out_recv, rows_f, states_f, stage,
    coef_a, coef_b, coef_g, coef_r, coef_u, xh, pre, carry, w_big, w_sum, w_part, w_pair, w_recv, w_total, w_all,
    ask_ss, ask_rs, x_ss, x_rs, agg_ss, agg_rs, out_ss, out_rs, w1_ss, w1_rs, w2_ss, w2_rs, pair_s, local_s,
):
    me_o = lax.axis_index("outer")
    me_g = lax.axis_index("grp")
    me = me_o * GRP + me_g

    grps = [lax.rem(me_g + q, GRP) for q in range(GRP)]

    def ahead(i):
        return lax.rem(me_o + lax.rem(i * STRIDE, OUTER), OUTER)

    def behind(i):
        return lax.rem(me_o + OUTER - lax.rem(i * STRIDE, OUTER), OUTER)

    def to_others(act):
        for q in range(1, GRP):
            act(me_o, grps[q])

        def body(i, _):
            o = ahead(i)
            for q in range(GRP):
                act(o, grps[q])
            return 0

        lax.fori_loop(1, OUTER, body, 0)

    def send(src, dst, send_sem, recv_sem, o, g):
        pltpu.make_async_remote_copy(
            src_ref=src, dst_ref=dst, send_sem=send_sem, recv_sem=recv_sem,
            device_id=(o, g), device_id_type=MESH,
        ).start()

    def done(ref, sem):
        pltpu.make_async_copy(ref, ref, sem).wait()

    barrier = pltpu.get_barrier_semaphore()
    to_others(
        lambda o, g: pl.semaphore_signal(barrier, inc=1, device_id=(o, g), device_id_type=MESH)
    )

    def upper_block(b, _):
        r = pl.multiple_of(b * 128, 128)
        upper[pl.ds(r, 128), :] = jnp.where(
            iota((128, PATHS), 0) + r < iota((128, PATHS), 1), 1.0, 0.0
        ).astype(BF16)
        return 0

    lax.fori_loop(0, PATHS // 128, upper_block, 0)
    owner_v[...] = ((ids_ref[...] >> 8) * 171) >> 9
    asks[...] = jnp.zeros_like(asks)

    def index_hop(t, base):
        own = owner_v[pl.ds(t, 1), :]
        local = ids_ref[pl.ds(t, 1), :] - own * LINKS + 1
        hot = iota((DEV, PATHS), 0) == own
        hot_b = jnp.where(hot, 1.0, 0.0).astype(BF16)
        before = jnp.dot(hot_b, upper[...], preferred_element_type=F32) + base
        rank = jnp.sum(jnp.where(hot, before, 0.0), axis=0, keepdims=True).astype(I32)
        slot = jnp.clip(own * CAP + rank, 0, DEV * CAP - 1)
        slot_v[pl.ds(pl.multiple_of(t * PATHS, PATHS), PATHS)] = slot.reshape(PATHS)
        at_rank = iota((128, PATHS), 0) == rank
        pos = iota((1, PATHS), 1) + t * PATHS

        def parts(row, bits):
            high = (row >> bits).astype(F32)
            low = (row & ((1 << bits) - 1)).astype(F32)
            both = jnp.concatenate(
                [jnp.where(at_rank, high, 0.0), jnp.where(at_rank, low, 0.0)], axis=0
            ).astype(BF16)
            return lax.dot_general(hot_b, both, NT, preferred_element_type=F32)

        asks[:, :256] += parts(local, 5)
        asks[:, 256:] += parts(pos, 7)
        return base + jnp.sum(jnp.where(hot, 1.0, 0.0), axis=1, keepdims=True)

    lax.fori_loop(0, HOPS, index_hop, jnp.zeros((DEV, 1), F32))
    ask_rows[...] = (asks[:, :128] * 32.0 + asks[:, 128:256]).astype(I32)
    pos = (asks[:, 256:384] * 128.0 + asks[:, 384:]).astype(I32)
    pos_rows[...] = jnp.clip(pos, 0, ROWS - 1)

    def spread(o, _):
        ask_send[o] = ask_rows[pl.ds(o, 1), :]
        pos = pos_rows[pl.ds(o, 1), :]
        pos_v[pl.ds(pl.multiple_of(o * 128, 128), 128)] = pos.reshape(128)
        return 0

    lax.fori_loop(0, DEV, spread, 0)
    to_slots = pltpu.make_async_copy(slot_v, slot_s, local_s.at[0])
    to_pos = pltpu.make_async_copy(pos_v, pos_s, local_s.at[1])
    to_slots.start()
    to_pos.start()

    ask_recv[me] = ask_send[me]
    pl.semaphore_wait(barrier, DEV - 1)

    to_others(
        lambda o, g: send(ask_send.at[o * GRP + g], ask_recv.at[me], ask_ss, ask_rs, o, g)
    )

    table[:, :WIDTH] = link_ref[...]
    table[:, WIDTH:] = agg_ref[...]

    def widen(b, _):
        r = pl.multiple_of(b * 64, 64)
        block = states_ref[pl.ds(r, 64)].astype(F32)
        states_f[pl.ds(pl.multiple_of(b * 512, 512), 512), :] = block.reshape(512, WIDTH)
        return 0

    lax.fori_loop(0, PATHS // 64, widen, 0)
    carry[...] = final_ref[...].astype(F32)
    third = 2 * WIDTH
    none = jnp.zeros((WIDTH, WIDTH), BF16)
    w_big[:WIDTH, : 3 * WIDTH] = w_in_ref[...]
    w_big[:WIDTH, 3 * WIDTH :] = none
    w_big[WIDTH:, :third] = w_rec_ref[:, :third]
    w_big[WIDTH:, third : 3 * WIDTH] = none
    w_big[WIDTH:, 3 * WIDTH :] = w_rec_ref[:, third:]
    b_in = b_in_ref[...].reshape(1, 3 * WIDTH)
    b_rec = b_rec_ref[...].reshape(1, 3 * WIDTH)
    bias = jnp.concatenate(
        [b_in[:, :third] + b_rec[:, :third], b_in[:, third:], b_rec[:, third:]], axis=1
    )
    to_slots.wait()
    to_pos.wait()

    done(ask_recv.at[pl.ds(0, DEV - 1)], ask_rs)
    ask_cols[...] = jnp.transpose((ask_recv[...].reshape(DEV, 128) - 1).astype(F32))

    def answer(i, first):
        o = ahead(i)
        cols = []
        for g in range(GRP):
            mine = jnp.where(iota((CAP, 128), 1) == o * GRP + g, ask_cols[:CAP, :], 0.0)
            cols.append(jnp.sum(mine, axis=1, keepdims=True))
        col = jnp.concatenate(cols, axis=0).astype(I32)
        hot = jnp.where(iota((GRP * CAP, LINKS), 1) == col, 1.0, 0.0).astype(BF16)
        got = jnp.dot(hot, table[...], preferred_element_type=F32)
        for g in range(GRP):
            x_send[o * GRP + g] = got[g * CAP : (g + 1) * CAP, :WIDTH].astype(BF16)
            agg_send[o * GRP + g] = got[g * CAP : (g + 1) * CAP, WIDTH:].astype(BF16)
        for q in range(first, GRP):
            p = o * GRP + grps[q]
            send(x_send.at[p], x_recv.at[me], x_ss, x_rs.at[me_o], o, grps[q])
        return 0

    answer(0, 1)
    lax.fori_loop(1, OUTER, lambda i, _: answer(i, 0), 0)
    x_recv[me] = x_send[me]
    agg_recv[me] = agg_send[me]

    def send_agg(o, first):
        for q in range(first, GRP):
            p = o * GRP + grps[q]
            send(agg_send.at[p], agg_recv.at[me], agg_ss, agg_rs.at[me_o], o, grps[q])

    def take(recv, recv_sem, i, own=False):
        o = me_o if own else behind(i)
        done(recv.at[pl.ds(o * GRP, GRP - 1 if own else GRP)], recv_sem.at[o])
        block = recv[pl.ds(o * GRP, GRP)].astype(F32).reshape(GRP * CAP, WIDTH)
        rows_f[pl.ds(pl.multiple_of(o * GRP * CAP, 8), GRP * CAP), :] = block
        return 0

    def to_path_order(t):
        def body(b, _):
            r = pl.multiple_of(b * 32, 32)
            got = [rows_f[pl.ds(slot_s[t * PATHS + r + j], 1), :] for j in range(32)]
            for j in range(32):
                stage[pl.ds(r + j, 1), :] = got[j]
            return 0

        lax.fori_loop(0, PATHS // 32, body, 0)

    half_way = OUTER // 2 + 1

    def take_and_send(i, _):
        take(x_recv, x_rs, i)
        send_agg(ahead(2 * (i - half_way) + 1), 0)
        send_agg(ahead(2 * (i - half_way) + 2), 0)
        return 0

    take(x_recv, x_rs, 0, own=True)
    lax.fori_loop(1, half_way, lambda i, _: take(x_recv, x_rs, i), 0)
    send_agg(me_o, 1)
    send_agg(ahead(OUTER - 1), 0)
    lax.fori_loop(half_way, OUTER, take_and_send, 0)

    def forward_hop(t, _):
        to_path_order(t)

        def chunk(c, _):
            r = pl.multiple_of(c * CHUNK, CHUNK)
            out = pl.ds(pl.multiple_of(t * PATHS + r, CHUNK), CHUNK)
            h = states_f[pl.ds(r * HOPS + t, CHUNK, stride=HOPS), :]
            xh[out, :WIDTH] = stage[pl.ds(r, CHUNK), :].astype(BF16)
            xh[out, WIDTH:] = h.astype(BF16)
            both = jnp.dot(xh[out, :], w_big[...], preferred_element_type=F32) + bias
            u = jax.nn.sigmoid(both[:, :WIDTH])
            r_gate = jax.nn.sigmoid(both[:, WIDTH : 2 * WIDTH])
            recur = both[:, 3 * WIDTH :]
            cand = jnp.tanh(both[:, 2 * WIDTH : 3 * WIDTH] + r_gate * recur)
            coef_a[out, :] = (1.0 - u) * (1.0 - cand * cand)
            coef_b[out, :] = (h - cand) * u * (1.0 - u)
            coef_g[out, :] = recur * r_gate * (1.0 - r_gate)
            coef_r[out, :] = r_gate
            coef_u[out, :] = u
            return 0

        lax.fori_loop(0, PATHS // CHUNK, chunk, 0)
        return 0

    lax.fori_loop(0, HOPS, forward_hop, 0)
    take(agg_recv, agg_rs, 0, own=True)
    lax.fori_loop(1, OUTER, lambda i, _: take(agg_recv, agg_rs, i), 0)
    grads = coef_a

    def backward_hop(i, _):
        t = HOPS - 1 - i
        to_path_order(t)

        def chunk(c, _):
            r = pl.multiple_of(c * CHUNK, CHUNK)
            here = pl.ds(r, CHUNK)
            out = pl.ds(pl.multiple_of(t * PATHS + r, CHUNK), CHUNK)
            cg = carry[here, :] + stage[here, :]
            pc = cg * coef_a[out, :]
            parts = [cg * coef_b[out, :], pc * coef_g[out, :], pc, pc * coef_r[out, :]]
            rounded = jnp.concatenate([part.astype(BF16) for part in parts], axis=1)
            pre[out, :] = rounded
            back = lax.dot_general(rounded, w_big[...], NT, preferred_element_type=F32)
            grads[out, :] = back[:, :WIDTH]
            carry[here, :] = cg * coef_u[out, :] + back[:, WIDTH:]
            return 0

        lax.fori_loop(0, PATHS // CHUNK, chunk, 0)
        return 0

    lax.fori_loop(0, HOPS, backward_hop, 0)

    def give(o, g):
        p = o * GRP + g
        for first in range(0, CAP, 24):
            got = [grads[pl.ds(pos_s[p * 128 + first + j], 1), :] for j in range(24)]
            for j in range(24):
                stage[pl.ds(first + j, 1), :] = got[j]
        out_send[p] = stage[:CAP, :].astype(BF16)

    def give_group(i, _):
        o = ahead(i)
        for q in range(GRP):
            give(o, grps[q])
            send(out_send.at[o * GRP + grps[q]], out_recv.at[me], out_ss, out_rs.at[me_o], o, grps[q])
        return 0

    def rows8(ref, n):
        return ref.at[pl.ds(pl.multiple_of(n * 8, 8), 8), :]

    core = lax.rem(me_o, 2)
    chip = me_o // 2
    seat = chip * GRP + me_g
    half = DEV // 2
    mine = pl.ds(pl.multiple_of(core * half * 8, 8), half * 8)
    theirs = pl.ds(pl.multiple_of((1 - core) * half * 8, 8), half * 8)
    twin = me_o + 1 - 2 * core

    def to_same_core(act):
        for q in range(1, GRP):
            act(chip, grps[q])

        def body(i, _):
            z = lax.rem(chip + lax.rem(i * 5, OUTER // 2), OUTER // 2)
            for q in range(GRP):
                act(z, grps[q])
            return 0

        lax.fori_loop(1, OUTER // 2, body, 0)

    lax.fori_loop(1, 6, give_group, 0)
    w_sum[...] = jnp.zeros_like(w_sum)

    def weights(c, sums):
        rows = pl.ds(pl.multiple_of(c * PATHS, PATHS), PATHS)
        w_sum[...] += lax.dot_general(xh[rows, :], pre[rows, :], TN, preferred_element_type=F32)
        return sums + jnp.sum(pre[rows, :].astype(F32), axis=0, keepdims=True)

    sums = lax.fori_loop(0, HOPS, weights, jnp.zeros((1, 4 * WIDTH), F32))

    w_rows = [w_sum[:WIDTH, r * WIDTH : (r + 1) * WIDTH] for r in (0, 1, 2)]
    w_rows += [w_sum[WIDTH:, r * WIDTH : (r + 1) * WIDTH] for r in (0, 1, 3)]
    for r in range(6):
        w_part[pl.ds(r, DEV, stride=8), :] = w_rows[r]
    bias8 = jnp.concatenate(
        [sums[:, r * WIDTH : (r + 1) * WIDTH] for r in (0, 1, 2, 0, 1, 3)]
        + [jnp.zeros((2, WIDTH), F32)],
        axis=0,
    )
    w_part[pl.ds(6, DEV, stride=8), :] = jnp.concatenate([bias8] * (DEV // 8), axis=0)
    w_part[pl.ds(7, DEV, stride=8), :] = jnp.zeros((DEV, WIDTH), F32)
    send(w_part.at[theirs, :], w_pair, pair_s.at[0], pair_s.at[1], twin, me_g)
    lax.fori_loop(6, 14, give_group, 0)
    done(w_pair, pair_s.at[1])
    w_pair[...] += w_part[mine, :]
    to_same_core(
        lambda z, g: send(
            rows8(w_pair, z * GRP + g), rows8(w_recv, seat), w1_ss, w1_rs, z * 2 + core, g
        )
    )
    lax.fori_loop(14, 26, give_group, 0)
    done(w_recv.at[pl.ds(0, (half - 1) * 8)], w1_rs)
    own_rows = pl.ds(pl.multiple_of(seat * 8, 8), 8)
    w_recv[own_rows, :] = w_pair[own_rows, :]
    total = jnp.sum(w_recv[...].reshape(half, 8, WIDTH), axis=0)
    total = total * (1.0 / math.sqrt(ROWS * DEV))
    w_total[...] = total
    line = core * half + seat
    to_same_core(
        lambda z, g: send(w_total, rows8(w_all, line), w2_ss, w2_rs, z * 2 + core, g)
    )
    w_all[pl.ds(pl.multiple_of(line * 8, 8), 8), :] = total
    lax.fori_loop(26, OUTER, give_group, 0)
    for q in range(1, GRP):
        give(me_o, grps[q])
        send(out_send.at[me_o * GRP + grps[q]], out_recv.at[me], out_ss, out_rs.at[me_o], me_o, grps[q])
    give(me_o, me_g)
    out_recv[me] = out_send[me]
    path_out[...] = carry[...].astype(BF16)

    link_out[...] = jnp.zeros_like(link_out)

    def collect(o):
        part = jnp.zeros((LINKS, WIDTH), F32)
        for g in range(GRP):
            p = o * GRP + g
            hot = jnp.where(iota((LINKS, 128), 0) == ask_recv[p] - 1, 1.0, 0.0).astype(BF16)
            part += jnp.dot(hot[:, :CAP], out_recv[p], preferred_element_type=F32)
        link_out[...] += part

    def collect_next(i, _):
        o = behind(i)
        done(out_recv.at[pl.ds(o * GRP, GRP)], out_rs.at[o])
        collect(o)
        return 0

    lax.fori_loop(1, OUTER // 2, collect_next, 0)
    done(w_all.at[pl.ds(0, (half - 1) * 8)], w2_rs)
    send(w_all.at[mine, :], w_all.at[mine, :], pair_s.at[2], pair_s.at[3], twin, me_g)
    lax.fori_loop(OUTER // 2, OUTER, collect_next, 0)
    done(out_recv.at[pl.ds(0, GRP - 1)], out_rs.at[me_o])
    collect(me_o)
    done(w_all.at[theirs, :], pair_s.at[3])
    for r in range(3):
        lanes = slice(r * WIDTH, (r + 1) * WIDTH)
        w_in_out[:, lanes] = w_all[pl.ds(r, DEV, stride=8), :]
        w_rec_out[:, lanes] = w_all[pl.ds(3 + r, DEV, stride=8), :]
    bias_out[...] = w_all[pl.ds(6, 8, stride=8), :]

    for buf, sem in (
        (ask_send, ask_ss), (x_send, x_ss), (agg_send, agg_ss), (out_send, out_ss)
    ):
        done(buf.at[pl.ds(0, DEV - 1)], sem)
    done(w_recv.at[pl.ds(0, (half - 1) * 8)], w1_ss)
    done(w_recv.at[pl.ds(0, (half - 1) * 8)], w2_ss)
    done(w_pair, pair_s.at[0])
    done(w_pair, pair_s.at[2])


def finish(path, link, w_in, w_rec, bias, path_out, link_out, w_in_out, w_rec_out, b_in_out, b_rec_out):
    path_out[...] = path[...]
    link_out[...] = link[...]
    w_in_out[...] = w_in[...]
    w_rec_out[...] = w_rec[...]
    for r in range(3):
        b_in_out[pl.ds(r * WIDTH, WIDTH)] = bias[r, :]
        b_rec_out[pl.ds(r * WIDTH, WIDTH)] = bias[3 + r, :]


def per_device(link_ids, path_states, final_grad, link_states, agg_grad, w_in, w_rec, b_in, b_rec):
    vmem = pl.BlockSpec(memory_space=pltpu.VMEM)
    one = pltpu.SemaphoreType.DMA
    some = pltpu.SemaphoreType.DMA((OUTER,))
    rows_pair = pltpu.VMEM((DEV, CAP, WIDTH), BF16)
    wide = pltpu.VMEM((ROWS, WIDTH), F32)
    shapes = (
        jax.ShapeDtypeStruct((PATHS, WIDTH), BF16),
        jax.ShapeDtypeStruct((LINKS, WIDTH), F32),
        jax.ShapeDtypeStruct((WIDTH, 3 * WIDTH), F32),
        jax.ShapeDtypeStruct((WIDTH, 3 * WIDTH), F32),
    )
    results = pl.pallas_call(
        kernel,
        out_shape=shapes + (jax.ShapeDtypeStruct((8, WIDTH), F32),),
        in_specs=[vmem] * 9,
        out_specs=(vmem,) * 5,
        scratch_shapes=[
            pltpu.VMEM((PATHS, PATHS), BF16),
            pltpu.VMEM((HOPS, PATHS), I32),
            pltpu.VMEM((ROWS,), I32),
            pltpu.VMEM((DEV, 512), F32),
            pltpu.VMEM((DEV, 128), I32),
            pltpu.VMEM((DEV, 128), I32),
            pltpu.VMEM((DEV, 1, 128), I32),
            pltpu.VMEM((DEV, 1, 128), I32),
            pltpu.VMEM((128, DEV), F32),
            pltpu.VMEM((DEV * 128,), I32),
            pltpu.SMEM((ROWS,), I32),
            pltpu.SMEM((DEV * 128,), I32),
            pltpu.VMEM((LINKS, 2 * WIDTH), BF16),
            rows_pair, rows_pair, rows_pair, rows_pair, rows_pair, rows_pair,
            pltpu.VMEM((DEV * CAP, WIDTH), F32),
            pltpu.VMEM((ROWS + 8, WIDTH), F32),
            pltpu.VMEM((PATHS, WIDTH), F32),
            wide, wide, wide, wide, wide,
            pltpu.VMEM((ROWS, 2 * WIDTH), BF16),
            pltpu.VMEM((ROWS, 4 * WIDTH), BF16),
            pltpu.VMEM((PATHS, WIDTH), F32),
            pltpu.VMEM((2 * WIDTH, 4 * WIDTH), BF16),
            pltpu.VMEM((2 * WIDTH, 4 * WIDTH), F32),
            pltpu.VMEM((DEV * 8 + 8, WIDTH), F32),
            pltpu.VMEM((DEV * 4, WIDTH), F32),
            pltpu.VMEM((DEV * 4, WIDTH), F32),
            pltpu.VMEM((8, WIDTH), F32),
            pltpu.VMEM((DEV * 8 + 8, WIDTH), F32),
        ] + [one, one, one, some, one, some, one, some, one, one, one, one]
        + [pltpu.SemaphoreType.DMA((4,)), pltpu.SemaphoreType.DMA((2,))],
        compiler_params=pltpu.CompilerParams(
            collective_id=0, has_side_effects=True, vmem_limit_bytes=60 * 2**20
        ),
    )(
        jnp.transpose(link_ids), path_states, final_grad, link_states, agg_grad, w_in, w_rec,
        b_in, b_rec,
    )
    flat = jax.ShapeDtypeStruct((3 * WIDTH,), F32)
    return pl.pallas_call(
        finish,
        out_shape=shapes + (flat, flat),
        in_specs=[vmem] * 5,
        out_specs=(vmem,) * 6,
    )(*results)


def solution(mesh):
    rows = P(("outer", "grp"), None)
    return jax.shard_map(
        per_device,
        mesh=mesh,
        in_specs=(rows, P(("outer", "grp"), None, None), rows, rows, rows, P(), P(), P(), P()),
        out_specs=(rows, rows, P(), P(), P(), P()),
        check_vma=False,
    )
```

```python
import functools
import math

import jax
import jax.numpy as jnp
from jax import lax
from jax.experimental import pallas as pl
from jax.experimental.pallas import tpu as pltpu
from jax.sharding import PartitionSpec as P

MESH = pl.DeviceIdType.MESH
F32 = jnp.float32
BF16 = jnp.bfloat16
I32 = jnp.int32

OUTER = 32
GRP = 4
DEV = OUTER * GRP
HOPS = 8
PATHS = 768
LINKS = 768
WIDTH = 128
ROWS = PATHS * HOPS
CAP = 3 * ROWS // (2 * DEV)
STRIDE = 11
CHUNK = 768
NT = (((1,), (1,)), ((), ()))
TN = (((0,), (0,)), ((), ()))


def iota(shape, dim):
    return lax.broadcasted_iota(I32, shape, dim)


def kernel(
    ids_ref, states_ref, final_ref, link_ref, agg_ref, w_in_ref, w_rec_ref, b_in_ref, b_rec_ref,
    path_out, link_out, w_in_out, w_rec_out, bias_out,
    upper, owner_v, slot_v, asks, ask_rows, pos_rows, ask_send, ask_recv, ask_cols, pos_v, slot_s, pos_s, table,
    x_send, agg_send, x_recv, agg_recv, out_send, out_recv, rows_f, states_f, stage,
    coef_a, coef_b, coef_g, coef_r, coef_u, xh, pre, carry, w_big, w_sum, w_part, w_pair, w_recv, w_total, w_all, all_b,
    ask_ss, ask_rs, x_ss, x_rs, agg_ss, agg_rs, out_ss, out_rs, w1_ss, w1_rs, w2_ss, w2_rs, pair_s, local_s,
):
    me_o = lax.axis_index("outer")
    me_g = lax.axis_index("grp")
    me = me_o * GRP + me_g

    grps = [lax.rem(me_g + q, GRP) for q in range(GRP)]

    def ahead(i):
        return lax.rem(me_o + lax.rem(i * STRIDE, OUTER), OUTER)

    def behind(i):
        return lax.rem(me_o + OUTER - lax.rem(i * STRIDE, OUTER), OUTER)

    def to_others(act):
        for q in range(1, GRP):
            act(me_o, grps[q])

        def body(i, _):
            o = ahead(i)
            for q in range(GRP):
                act(o, grps[q])
            return 0

        lax.fori_loop(1, OUTER, body, 0)

    def send(src, dst, send_sem, recv_sem, o, g):
        pltpu.make_async_remote_copy(
            src_ref=src, dst_ref=dst, send_sem=send_sem, recv_sem=recv_sem,
            device_id=(o, g), device_id_type=MESH,
        ).start()

    def done(ref, sem):
        pltpu.make_async_copy(ref, ref, sem).wait()

    barrier = pltpu.get_barrier_semaphore()
    to_others(
        lambda o, g: pl.semaphore_signal(barrier, inc=1, device_id=(o, g), device_id_type=MESH)
    )

    def upper_block(b, _):
        r = pl.multiple_of(b * 128, 128)
        upper[pl.ds(r, 128), :] = jnp.where(
            iota((128, PATHS), 0) + r < iota((128, PATHS), 1), 1.0, 0.0
        ).astype(BF16)
        return 0

    lax.fori_loop(0, PATHS // 128, upper_block, 0)
    owner_v[...] = ((ids_ref[...] >> 8) * 171) >> 9
    asks[...] = jnp.zeros_like(asks)

    def index_hop(t, base):
        own = owner_v[pl.ds(t, 1), :]
        local = ids_ref[pl.ds(t, 1), :] - own * LINKS + 1
        hot = iota((DEV, PATHS), 0) == own
        hot_b = jnp.where(hot, 1.0, 0.0).astype(BF16)
        before = jnp.dot(hot_b, upper[...], preferred_element_type=F32) + base
        rank = jnp.sum(jnp.where(hot, before, 0.0), axis=0, keepdims=True).astype(I32)
        slot = jnp.clip(own * CAP + rank, 0, DEV * CAP - 1)
        slot_v[pl.ds(pl.multiple_of(t * PATHS, PATHS), PATHS)] = slot.reshape(PATHS)
        at_rank = iota((128, PATHS), 0) == rank
        pos = iota((1, PATHS), 1) + t * PATHS

        def parts(row, bits):
            high = (row >> bits).astype(F32)
            low = (row & ((1 << bits) - 1)).astype(F32)
            both = jnp.concatenate(
                [jnp.where(at_rank, high, 0.0), jnp.where(at_rank, low, 0.0)], axis=0
            ).astype(BF16)
            return lax.dot_general(hot_b, both, NT, preferred_element_type=F32)

        asks[:, :256] += parts(local, 5)
        asks[:, 256:] += parts(pos, 7)
        return base + jnp.sum(jnp.where(hot, 1.0, 0.0), axis=1, keepdims=True)

    lax.fori_loop(0, HOPS, index_hop, jnp.zeros((DEV, 1), F32))
    ask_rows[...] = (asks[:, :128] * 32.0 + asks[:, 128:256]).astype(I32)
    pos = (asks[:, 256:384] * 128.0 + asks[:, 384:]).astype(I32)
    pos_rows[...] = jnp.clip(pos, 0, ROWS - 1)

    def spread(o, _):
        ask_send[o] = ask_rows[pl.ds(o, 1), :]
        pos = pos_rows[pl.ds(o, 1), :]
        pos_v[pl.ds(pl.multiple_of(o * 128, 128), 128)] = pos.reshape(128)
        return 0

    lax.fori_loop(0, DEV, spread, 0)
    to_slots = pltpu.make_async_copy(slot_v, slot_s, local_s.at[0])
    to_pos = pltpu.make_async_copy(pos_v, pos_s, local_s.at[1])
    to_slots.start()
    to_pos.start()

    ask_recv[me] = ask_send[me]
    pl.semaphore_wait(barrier, DEV - 1)

    to_others(
        lambda o, g: send(ask_send.at[o * GRP + g], ask_recv.at[me], ask_ss, ask_rs, o, g)
    )

    table[:, :WIDTH] = link_ref[...]
    table[:, WIDTH:] = agg_ref[...]

    def widen(b, _):
        r = pl.multiple_of(b * 64, 64)
        block = states_ref[pl.ds(r, 64)].astype(F32)
        states_f[pl.ds(pl.multiple_of(b * 512, 512), 512), :] = block.reshape(512, WIDTH)
        return 0

    lax.fori_loop(0, PATHS // 64, widen, 0)
    carry[...] = final_ref[...].astype(F32)
    third = 2 * WIDTH
    none = jnp.zeros((WIDTH, WIDTH), BF16)
    w_big[:WIDTH, : 3 * WIDTH] = w_in_ref[...]
    w_big[:WIDTH, 3 * WIDTH :] = none
    w_big[WIDTH:, :third] = w_rec_ref[:, :third]
    w_big[WIDTH:, third : 3 * WIDTH] = none
    w_big[WIDTH:, 3 * WIDTH :] = w_rec_ref[:, third:]
    b_in = b_in_ref[...].reshape(1, 3 * WIDTH)
    b_rec = b_rec_ref[...].reshape(1, 3 * WIDTH)
    bias = jnp.concatenate(
        [b_in[:, :third] + b_rec[:, :third], b_in[:, third:], b_rec[:, third:]], axis=1
    )
    to_slots.wait()
    to_pos.wait()

    done(ask_recv.at[pl.ds(0, DEV - 1)], ask_rs)
    ask_cols[...] = jnp.transpose((ask_recv[...].reshape(DEV, 128) - 1).astype(F32))

    def answer(i, first):
        o = ahead(i)
        cols = []
        for g in range(GRP):
            mine = jnp.where(iota((CAP, 128), 1) == o * GRP + g, ask_cols[:CAP, :], 0.0)
            cols.append(jnp.sum(mine, axis=1, keepdims=True))
        col = jnp.concatenate(cols, axis=0).astype(I32)
        hot = jnp.where(iota((GRP * CAP, LINKS), 1) == col, 1.0, 0.0).astype(BF16)
        got = jnp.dot(hot, table[...], preferred_element_type=F32)
        for g in range(GRP):
            x_send[o * GRP + g] = got[g * CAP : (g + 1) * CAP, :WIDTH].astype(BF16)
            agg_send[o * GRP + g] = got[g * CAP : (g + 1) * CAP, WIDTH:].astype(BF16)
        for q in range(first, GRP):
            p = o * GRP + grps[q]
            send(x_send.at[p], x_recv.at[me], x_ss, x_rs.at[me_o], o, grps[q])
        return 0

    answer(0, 1)
    lax.fori_loop(1, OUTER, lambda i, _: answer(i, 0), 0)
    x_recv[me] = x_send[me]
    agg_recv[me] = agg_send[me]

    def send_agg(o, first):
        for q in range(first, GRP):
            p = o * GRP + grps[q]
            send(agg_send.at[p], agg_recv.at[me], agg_ss, agg_rs.at[me_o], o, grps[q])

    def take(recv, recv_sem, i, own=False):
        o = me_o if own else behind(i)
        done(recv.at[pl.ds(o * GRP, GRP - 1 if own else GRP)], recv_sem.at[o])
        block = recv[pl.ds(o * GRP, GRP)].astype(F32).reshape(GRP * CAP, WIDTH)
        rows_f[pl.ds(pl.multiple_of(o * GRP * CAP, 8), GRP * CAP), :] = block
        return 0

    def to_path_order(t):
        def body(b, _):
            r = pl.multiple_of(b * 32, 32)
            got = [rows_f[pl.ds(slot_s[t * PATHS + r + j], 1), :] for j in range(32)]
            for j in range(32):
                stage[pl.ds(r + j, 1), :] = got[j]
            return 0

        lax.fori_loop(0, PATHS // 32, body, 0)

    half_way = OUTER // 2 + 1

    def take_and_send(i, _):
        take(x_recv, x_rs, i)
        send_agg(ahead(2 * (i - half_way) + 1), 0)
        send_agg(ahead(2 * (i - half_way) + 2), 0)
        return 0

    take(x_recv, x_rs, 0, own=True)
    lax.fori_loop(1, half_way, lambda i, _: take(x_recv, x_rs, i), 0)
    send_agg(me_o, 1)
    send_agg(ahead(OUTER - 1), 0)
    lax.fori_loop(half_way, OUTER, take_and_send, 0)

    def forward_hop(t, _):
        to_path_order(t)

        def chunk(c, _):
            r = pl.multiple_of(c * CHUNK, CHUNK)
            out = pl.ds(pl.multiple_of(t * PATHS + r, CHUNK), CHUNK)
            h = states_f[pl.ds(r * HOPS + t, CHUNK, stride=HOPS), :]
            xh[out, :WIDTH] = stage[pl.ds(r, CHUNK), :].astype(BF16)
            xh[out, WIDTH:] = h.astype(BF16)
            both = jnp.dot(xh[out, :], w_big[...], preferred_element_type=F32) + bias
            u = jax.nn.sigmoid(both[:, :WIDTH])
            r_gate = jax.nn.sigmoid(both[:, WIDTH : 2 * WIDTH])
            recur = both[:, 3 * WIDTH :]
            cand = jnp.tanh(both[:, 2 * WIDTH : 3 * WIDTH] + r_gate * recur)
            coef_a[out, :] = (1.0 - u) * (1.0 - cand * cand)
            coef_b[out, :] = (h - cand) * u * (1.0 - u)
            coef_g[out, :] = recur * r_gate * (1.0 - r_gate)
            coef_r[out, :] = r_gate
            coef_u[out, :] = u
            return 0

        lax.fori_loop(0, PATHS // CHUNK, chunk, 0)
        return 0

    lax.fori_loop(0, HOPS, forward_hop, 0)
    take(agg_recv, agg_rs, 0, own=True)
    lax.fori_loop(1, OUTER, lambda i, _: take(agg_recv, agg_rs, i), 0)
    grads = coef_a

    def backward_hop(i, _):
        t = HOPS - 1 - i
        to_path_order(t)

        def chunk(c, _):
            r = pl.multiple_of(c * CHUNK, CHUNK)
            here = pl.ds(r, CHUNK)
            out = pl.ds(pl.multiple_of(t * PATHS + r, CHUNK), CHUNK)
            cg = carry[here, :] + stage[here, :]
            pc = cg * coef_a[out, :]
            parts = [cg * coef_b[out, :], pc * coef_g[out, :], pc, pc * coef_r[out, :]]
            rounded = jnp.concatenate([part.astype(BF16) for part in parts], axis=1)
            pre[out, :] = rounded
            back = lax.dot_general(rounded, w_big[...], NT, preferred_element_type=F32)
            grads[out, :] = back[:, :WIDTH]
            carry[here, :] = cg * coef_u[out, :] + back[:, WIDTH:]
            return 0

        lax.fori_loop(0, PATHS // CHUNK, chunk, 0)
        return 0

    lax.fori_loop(0, HOPS, backward_hop, 0)

    def give(o, g):
        p = o * GRP + g
        for first in range(0, CAP, 24):
            got = [grads[pl.ds(pos_s[p * 128 + first + j], 1), :] for j in range(24)]
            for j in range(24):
                stage[pl.ds(first + j, 1), :] = got[j]
        out_send[p] = stage[:CAP, :].astype(BF16)

    def give_group(i, _):
        o = ahead(i)
        for q in range(GRP):
            give(o, grps[q])
            send(out_send.at[o * GRP + grps[q]], out_recv.at[me], out_ss, out_rs.at[me_o], o, grps[q])
        return 0

    def rows8(ref, n):
        return ref.at[pl.ds(pl.multiple_of(n * 8, 8), 8), :]

    core = lax.rem(me_o, 2)
    chip = me_o // 2
    seat = chip * GRP + me_g
    half = DEV // 2
    mine = pl.ds(pl.multiple_of(core * half * 8, 8), half * 8)
    theirs = pl.ds(pl.multiple_of((1 - core) * half * 8, 8), half * 8)
    twin = me_o + 1 - 2 * core

    def to_same_core(act):
        for q in range(1, GRP):
            act(chip, grps[q])

        def body(i, _):
            z = lax.rem(chip + lax.rem(i * 5, OUTER // 2), OUTER // 2)
            for q in range(GRP):
                act(z, grps[q])
            return 0

        lax.fori_loop(1, OUTER // 2, body, 0)

    lax.fori_loop(1, 4, give_group, 0)
    w_sum[...] = jnp.zeros_like(w_sum)

    def weights(c, sums):
        rows = pl.ds(pl.multiple_of(c * PATHS, PATHS), PATHS)
        w_sum[...] += lax.dot_general(xh[rows, :], pre[rows, :], TN, preferred_element_type=F32)
        return sums + jnp.sum(pre[rows, :].astype(F32), axis=0, keepdims=True)

    sums = lax.fori_loop(0, HOPS, weights, jnp.zeros((1, 4 * WIDTH), F32))

    w_rows = [w_sum[:WIDTH, r * WIDTH : (r + 1) * WIDTH] for r in (0, 1, 2)]
    w_rows += [w_sum[WIDTH:, r * WIDTH : (r + 1) * WIDTH] for r in (0, 1, 3)]
    for r in range(6):
        w_part[pl.ds(r, DEV, stride=8), :] = w_rows[r]
    bias8 = jnp.concatenate(
        [sums[:, r * WIDTH : (r + 1) * WIDTH] for r in (0, 1, 2, 0, 1, 3)]
        + [jnp.zeros((2, WIDTH), F32)],
        axis=0,
    )
    w_part[pl.ds(6, DEV, stride=8), :] = jnp.concatenate([bias8] * (DEV // 8), axis=0)
    w_part[pl.ds(7, DEV, stride=8), :] = jnp.zeros((DEV, WIDTH), F32)
    send(w_part.at[theirs, :], w_pair, pair_s.at[0], pair_s.at[1], twin, me_g)
    lax.fori_loop(4, 7, give_group, 0)
    done(w_pair, pair_s.at[1])
    w_pair[...] += w_part[mine, :]
    to_same_core(
        lambda z, g: send(
            rows8(w_pair, z * GRP + g), rows8(w_recv, seat), w1_ss, w1_rs, z * 2 + core, g
        )
    )
    lax.fori_loop(7, 16, give_group, 0)
    done(w_recv.at[pl.ds(0, (half - 1) * 8)], w1_rs)
    own_rows = pl.ds(pl.multiple_of(seat * 8, 8), 8)
    w_recv[own_rows, :] = w_pair[own_rows, :]
    total = jnp.sum(w_recv[...].reshape(half, 8, WIDTH), axis=0)
    total = total * (1.0 / math.sqrt(ROWS * DEV))
    w_total[...] = total.astype(BF16)
    line = core * half + seat
    to_same_core(
        lambda z, g: send(w_total, all_b.at[line], w2_ss, w2_rs, z * 2 + core, g)
    )
    all_b[line] = w_total[...]
    lax.fori_loop(16, OUTER, give_group, 0)
    for q in range(1, GRP):
        give(me_o, grps[q])
        send(out_send.at[me_o * GRP + grps[q]], out_recv.at[me], out_ss, out_rs.at[me_o], me_o, grps[q])
    give(me_o, me_g)
    out_recv[me] = out_send[me]
    path_out[...] = carry[...].astype(BF16)

    link_out[...] = jnp.zeros_like(link_out)

    def collect(o):
        part = jnp.zeros((LINKS, WIDTH), F32)
        for g in range(GRP):
            p = o * GRP + g
            hot = jnp.where(iota((LINKS, 128), 0) == ask_recv[p] - 1, 1.0, 0.0).astype(BF16)
            part += jnp.dot(hot[:, :CAP], out_recv[p], preferred_element_type=F32)
        link_out[...] += part

    def collect_next(i, _):
        o = behind(i)
        done(out_recv.at[pl.ds(o * GRP, GRP)], out_rs.at[o])
        collect(o)
        return 0

    lax.fori_loop(1, OUTER // 2, collect_next, 0)
    done(all_b.at[pl.ds(0, half - 1)], w2_rs)
    send(all_b.at[pl.ds(core * half, half)], all_b.at[pl.ds(core * half, half)], pair_s.at[2], pair_s.at[3], twin, me_g)
    lax.fori_loop(OUTER // 2, OUTER, collect_next, 0)
    done(out_recv.at[pl.ds(0, GRP - 1)], out_rs.at[me_o])
    collect(me_o)
    done(all_b.at[pl.ds((1 - core) * half, half)], pair_s.at[3])
    w_all[: DEV * 8, :] = all_b[...].astype(F32).reshape(DEV * 8, WIDTH)
    for r in range(3):
        lanes = slice(r * WIDTH, (r + 1) * WIDTH)
        w_in_out[:, lanes] = w_all[pl.ds(r, DEV, stride=8), :]
        w_rec_out[:, lanes] = w_all[pl.ds(3 + r, DEV, stride=8), :]
    bias_out[...] = w_all[pl.ds(6, 8, stride=8), :]

    for buf, sem in (
        (ask_send, ask_ss), (x_send, x_ss), (agg_send, agg_ss), (out_send, out_ss)
    ):
        done(buf.at[pl.ds(0, DEV - 1)], sem)
    done(w_recv.at[pl.ds(0, (half - 1) * 8)], w1_ss)
    done(all_b.at[pl.ds(0, half - 1)], w2_ss)
    done(w_pair, pair_s.at[0])
    done(all_b.at[pl.ds(0, half)], pair_s.at[2])


def finish(path, link, w_in, w_rec, bias, path_out, link_out, w_in_out, w_rec_out, b_in_out, b_rec_out):
    path_out[...] = path[...]
    link_out[...] = link[...]
    w_in_out[...] = w_in[...]
    w_rec_out[...] = w_rec[...]
    for r in range(3):
        b_in_out[pl.ds(r * WIDTH, WIDTH)] = bias[r, :]
        b_rec_out[pl.ds(r * WIDTH, WIDTH)] = bias[3 + r, :]


def per_device(link_ids, path_states, final_grad, link_states, agg_grad, w_in, w_rec, b_in, b_rec):
    vmem = pl.BlockSpec(memory_space=pltpu.VMEM)
    one = pltpu.SemaphoreType.DMA
    some = pltpu.SemaphoreType.DMA((OUTER,))
    rows_pair = pltpu.VMEM((DEV, CAP, WIDTH), BF16)
    wide = pltpu.VMEM((ROWS, WIDTH), F32)
    shapes = (
        jax.ShapeDtypeStruct((PATHS, WIDTH), BF16),
        jax.ShapeDtypeStruct((LINKS, WIDTH), F32),
        jax.ShapeDtypeStruct((WIDTH, 3 * WIDTH), F32),
        jax.ShapeDtypeStruct((WIDTH, 3 * WIDTH), F32),
    )
    results = pl.pallas_call(
        kernel,
        out_shape=shapes + (jax.ShapeDtypeStruct((8, WIDTH), F32),),
        in_specs=[vmem] * 9,
        out_specs=(vmem,) * 5,
        scratch_shapes=[
            pltpu.VMEM((PATHS, PATHS), BF16),
            pltpu.VMEM((HOPS, PATHS), I32),
            pltpu.VMEM((ROWS,), I32),
            pltpu.VMEM((DEV, 512), F32),
            pltpu.VMEM((DEV, 128), I32),
            pltpu.VMEM((DEV, 128), I32),
            pltpu.VMEM((DEV, 1, 128), I32),
            pltpu.VMEM((DEV, 1, 128), I32),
            pltpu.VMEM((128, DEV), F32),
            pltpu.VMEM((DEV * 128,), I32),
            pltpu.SMEM((ROWS,), I32),
            pltpu.SMEM((DEV * 128,), I32),
            pltpu.VMEM((LINKS, 2 * WIDTH), BF16),
            rows_pair, rows_pair, rows_pair, rows_pair, rows_pair, rows_pair,
            pltpu.VMEM((DEV * CAP, WIDTH), F32),
            pltpu.VMEM((ROWS + 8, WIDTH), F32),
            pltpu.VMEM((PATHS, WIDTH), F32),
            wide, wide, wide, wide, wide,
            pltpu.VMEM((ROWS, 2 * WIDTH), BF16),
            pltpu.VMEM((ROWS, 4 * WIDTH), BF16),
            pltpu.VMEM((PATHS, WIDTH), F32),
            pltpu.VMEM((2 * WIDTH, 4 * WIDTH), BF16),
            pltpu.VMEM((2 * WIDTH, 4 * WIDTH), F32),
            pltpu.VMEM((DEV * 8 + 8, WIDTH), F32),
            pltpu.VMEM((DEV * 4, WIDTH), F32),
            pltpu.VMEM((DEV * 4, WIDTH), F32),
            pltpu.VMEM((8, WIDTH), BF16),
            pltpu.VMEM((DEV * 8 + 8, WIDTH), F32),
            pltpu.VMEM((DEV, 8, WIDTH), BF16),
        ] + [one, one, one, some, one, some, one, some, one, one, one, one]
        + [pltpu.SemaphoreType.DMA((4,)), pltpu.SemaphoreType.DMA((2,))],
        compiler_params=pltpu.CompilerParams(
            collective_id=0, has_side_effects=True, vmem_limit_bytes=60 * 2**20
        ),
    )(
        jnp.transpose(link_ids), path_states, final_grad, link_states, agg_grad, w_in, w_rec,
        b_in, b_rec,
    )
    flat = jax.ShapeDtypeStruct((3 * WIDTH,), F32)
    return pl.pallas_call(
        finish,
        out_shape=shapes + (flat, flat),
        in_specs=[vmem] * 5,
        out_specs=(vmem,) * 6,
    )(*results)


def solution(mesh):
    rows = P(("outer", "grp"), None)
    return jax.shard_map(
        per_device,
        mesh=mesh,
        in_specs=(rows, P(("outer", "grp"), None, None), rows, rows, rows, P(), P(), P(), P()),
        out_specs=(rows, rows, P(), P(), P(), P()),
        check_vma=False,
    )
```

```python
import functools
import math

import jax
import jax.numpy as jnp
from jax import lax
from jax.experimental import pallas as pl
from jax.experimental.pallas import tpu as pltpu
from jax.sharding import PartitionSpec as P

MESH = pl.DeviceIdType.MESH
F32 = jnp.float32
BF16 = jnp.bfloat16
I32 = jnp.int32

OUTER = 32
GRP = 4
DEV = OUTER * GRP
HOPS = 8
PATHS = 768
LINKS = 768
WIDTH = 128
ROWS = PATHS * HOPS
CAP = 3 * ROWS // (2 * DEV)
STRIDE = 11
CHUNK = 768
NT = (((1,), (1,)), ((), ()))
TN = (((0,), (0,)), ((), ()))


def iota(shape, dim):
    return lax.broadcasted_iota(I32, shape, dim)


def kernel(
    ids_ref, states_ref, final_ref, link_ref, agg_ref, w_in_ref, w_rec_ref, b_in_ref, b_rec_ref,
    path_out, link_out, w_in_out, w_rec_out, bias_out,
    upper, owner_v, slot_v, asks, ask_rows, pos_rows, ask_send, ask_recv, ask_cols, pos_v, slot_s, pos_s, table,
    x_send, agg_send, x_recv, agg_recv, out_send, out_recv, rows_f, states_f, stage,
    coef_a, coef_b, coef_g, coef_r, coef_u, xh, pre, carry, w_big, w_sum, w_part, w_pair, w_recv, w_total, w_all, all_b,
    ask_ss, ask_rs, x_ss, x_rs, agg_ss, agg_rs, out_ss, out_rs, w1_ss, w1_rs, w2_ss, w2_rs, pair_s, local_s,
):
    me_o = lax.axis_index("outer")
    me_g = lax.axis_index("grp")
    me = me_o * GRP + me_g

    grps = [lax.rem(me_g + q, GRP) for q in range(GRP)]

    def ahead(i):
        return lax.rem(me_o + lax.rem(i * STRIDE, OUTER), OUTER)

    def behind(i):
        return lax.rem(me_o + OUTER - lax.rem(i * STRIDE, OUTER), OUTER)

    def to_others(act):
        for q in range(1, GRP):
            act(me_o, grps[q])

        def body(i, _):
            o = ahead(i)
            for q in range(GRP):
                act(o, grps[q])
            return 0

        lax.fori_loop(1, OUTER, body, 0)

    def send(src, dst, send_sem, recv_sem, o, g):
        pltpu.make_async_remote_copy(
            src_ref=src, dst_ref=dst, send_sem=send_sem, recv_sem=recv_sem,
            device_id=(o, g), device_id_type=MESH,
        ).start()

    def done(ref, sem):
        pltpu.make_async_copy(ref, ref, sem).wait()

    barrier = pltpu.get_barrier_semaphore()
    to_others(
        lambda o, g: pl.semaphore_signal(barrier, inc=1, device_id=(o, g), device_id_type=MESH)
    )

    def upper_block(b, _):
        r = pl.multiple_of(b * 128, 128)
        upper[pl.ds(r, 128), :] = jnp.where(
            iota((128, PATHS), 0) + r < iota((128, PATHS), 1), 1.0, 0.0
        ).astype(BF16)
        return 0

    lax.fori_loop(0, PATHS // 128, upper_block, 0)
    owner_v[...] = ((ids_ref[...] >> 8) * 171) >> 9
    asks[...] = jnp.zeros_like(asks)

    def index_hop(t, base):
        own = owner_v[pl.ds(t, 1), :]
        local = ids_ref[pl.ds(t, 1), :] - own * LINKS + 1
        hot = iota((DEV, PATHS), 0) == own
        hot_b = jnp.where(hot, 1.0, 0.0).astype(BF16)
        before = jnp.dot(hot_b, upper[...], preferred_element_type=F32) + base
        rank = jnp.sum(jnp.where(hot, before, 0.0), axis=0, keepdims=True).astype(I32)
        slot = jnp.clip(own * CAP + rank, 0, DEV * CAP - 1)
        slot_v[pl.ds(pl.multiple_of(t * PATHS, PATHS), PATHS)] = slot.reshape(PATHS)
        at_rank = iota((128, PATHS), 0) == rank
        pos = iota((1, PATHS), 1) + t * PATHS

        def parts(row, bits):
            high = (row >> bits).astype(F32)
            low = (row & ((1 << bits) - 1)).astype(F32)
            both = jnp.concatenate(
                [jnp.where(at_rank, high, 0.0), jnp.where(at_rank, low, 0.0)], axis=0
            ).astype(BF16)
            return lax.dot_general(hot_b, both, NT, preferred_element_type=F32)

        asks[:, :256] += parts(local, 5)
        asks[:, 256:] += parts(pos, 7)
        return base + jnp.sum(jnp.where(hot, 1.0, 0.0), axis=1, keepdims=True)

    lax.fori_loop(0, HOPS, index_hop, jnp.zeros((DEV, 1), F32))
    ask_rows[...] = (asks[:, :128] * 32.0 + asks[:, 128:256]).astype(I32)
    pos = (asks[:, 256:384] * 128.0 + asks[:, 384:]).astype(I32)
    pos_rows[...] = jnp.clip(pos, 0, ROWS - 1)

    def spread(o, _):
        ask_send[o] = ask_rows[pl.ds(o, 1), :]
        pos = pos_rows[pl.ds(o, 1), :]
        pos_v[pl.ds(pl.multiple_of(o * 128, 128), 128)] = pos.reshape(128)
        return 0

    lax.fori_loop(0, DEV, spread, 0)
    to_slots = pltpu.make_async_copy(slot_v, slot_s, local_s.at[0])
    to_pos = pltpu.make_async_copy(pos_v, pos_s, local_s.at[1])
    to_slots.start()
    to_pos.start()

    ask_recv[me] = ask_send[me]
    pl.semaphore_wait(barrier, DEV - 1)

    to_others(
        lambda o, g: send(ask_send.at[o * GRP + g], ask_recv.at[me], ask_ss, ask_rs, o, g)
    )

    table[:, :WIDTH] = link_ref[...]
    table[:, WIDTH:] = agg_ref[...]

    def widen(b, _):
        r = pl.multiple_of(b * 64, 64)
        block = states_ref[pl.ds(r, 64)].astype(F32)
        states_f[pl.ds(pl.multiple_of(b * 512, 512), 512), :] = block.reshape(512, WIDTH)
        return 0

    lax.fori_loop(0, PATHS // 64, widen, 0)
    carry[...] = final_ref[...].astype(F32)
    third = 2 * WIDTH
    none = jnp.zeros((WIDTH, WIDTH), BF16)
    w_big[:WIDTH, : 3 * WIDTH] = w_in_ref[...]
    w_big[:WIDTH, 3 * WIDTH :] = none
    w_big[WIDTH:, :third] = w_rec_ref[:, :third]
    w_big[WIDTH:, third : 3 * WIDTH] = none
    w_big[WIDTH:, 3 * WIDTH :] = w_rec_ref[:, third:]
    b_in = b_in_ref[...].reshape(1, 3 * WIDTH)
    b_rec = b_rec_ref[...].reshape(1, 3 * WIDTH)
    bias = jnp.concatenate(
        [b_in[:, :third] + b_rec[:, :third], b_in[:, third:], b_rec[:, third:]], axis=1
    )
    to_slots.wait()
    to_pos.wait()

    done(ask_recv.at[pl.ds(0, DEV - 1)], ask_rs)
    ask_cols[...] = jnp.transpose((ask_recv[...].reshape(DEV, 128) - 1).astype(F32))

    def answer(i, first):
        o = ahead(i)
        cols = []
        for g in range(GRP):
            mine = jnp.where(iota((CAP, 128), 1) == o * GRP + g, ask_cols[:CAP, :], 0.0)
            cols.append(jnp.sum(mine, axis=1, keepdims=True))
        col = jnp.concatenate(cols, axis=0).astype(I32)
        hot = jnp.where(iota((GRP * CAP, LINKS), 1) == col, 1.0, 0.0).astype(BF16)
        got = jnp.dot(hot, table[...], preferred_element_type=F32)
        for g in range(GRP):
            x_send[o * GRP + g] = got[g * CAP : (g + 1) * CAP, :WIDTH].astype(BF16)
            agg_send[o * GRP + g] = got[g * CAP : (g + 1) * CAP, WIDTH:].astype(BF16)
        for q in range(first, GRP):
            p = o * GRP + grps[q]
            send(x_send.at[p], x_recv.at[me], x_ss, x_rs.at[me_o], o, grps[q])
        return 0

    answer(0, 1)
    lax.fori_loop(1, OUTER, lambda i, _: answer(i, 0), 0)
    x_recv[me] = x_send[me]
    agg_recv[me] = agg_send[me]

    def send_agg(o, first):
        for q in range(first, GRP):
            p = o * GRP + grps[q]
            send(agg_send.at[p], agg_recv.at[me], agg_ss, agg_rs.at[me_o], o, grps[q])

    def take(recv, recv_sem, i, own=False):
        o = me_o if own else behind(i)
        done(recv.at[pl.ds(o * GRP, GRP - 1 if own else GRP)], recv_sem.at[o])
        block = recv[pl.ds(o * GRP, GRP)].astype(F32).reshape(GRP * CAP, WIDTH)
        rows_f[pl.ds(pl.multiple_of(o * GRP * CAP, 8), GRP * CAP), :] = block
        return 0

    def to_path_order(t):
        def body(b, _):
            r = pl.multiple_of(b * 64, 64)
            got = [rows_f[pl.ds(slot_s[t * PATHS + r + j], 1), :] for j in range(64)]
            for j in range(64):
                stage[pl.ds(r + j, 1), :] = got[j]
            return 0

        lax.fori_loop(0, PATHS // 64, body, 0)

    half_way = OUTER // 2 + 1

    def take_and_send(i, _):
        take(x_recv, x_rs, i)
        send_agg(ahead(2 * (i - half_way) + 1), 0)
        send_agg(ahead(2 * (i - half_way) + 2), 0)
        return 0

    take(x_recv, x_rs, 0, own=True)
    lax.fori_loop(1, half_way, lambda i, _: take(x_recv, x_rs, i), 0)
    send_agg(me_o, 1)
    send_agg(ahead(OUTER - 1), 0)
    lax.fori_loop(half_way, OUTER, take_and_send, 0)

    def forward_hop(t, _):
        to_path_order(t)

        def chunk(c, _):
            r = pl.multiple_of(c * CHUNK, CHUNK)
            out = pl.ds(pl.multiple_of(t * PATHS + r, CHUNK), CHUNK)
            h = states_f[pl.ds(r * HOPS + t, CHUNK, stride=HOPS), :]
            xh[out, :WIDTH] = stage[pl.ds(r, CHUNK), :].astype(BF16)
            xh[out, WIDTH:] = h.astype(BF16)
            both = jnp.dot(xh[out, :], w_big[...], preferred_element_type=F32) + bias
            u = jax.nn.sigmoid(both[:, :WIDTH])
            r_gate = jax.nn.sigmoid(both[:, WIDTH : 2 * WIDTH])
            recur = both[:, 3 * WIDTH :]
            cand = jnp.tanh(both[:, 2 * WIDTH : 3 * WIDTH] + r_gate * recur)
            coef_a[out, :] = (1.0 - u) * (1.0 - cand * cand)
            coef_b[out, :] = (h - cand) * u * (1.0 - u)
            coef_g[out, :] = recur * r_gate * (1.0 - r_gate)
            coef_r[out, :] = r_gate
            coef_u[out, :] = u
            return 0

        lax.fori_loop(0, PATHS // CHUNK, chunk, 0)
        return 0

    lax.fori_loop(0, HOPS, forward_hop, 0)
    take(agg_recv, agg_rs, 0, own=True)
    lax.fori_loop(1, OUTER, lambda i, _: take(agg_recv, agg_rs, i), 0)
    grads = coef_a

    def backward_hop(i, _):
        t = HOPS - 1 - i
        to_path_order(t)

        def chunk(c, _):
            r = pl.multiple_of(c * CHUNK, CHUNK)
            here = pl.ds(r, CHUNK)
            out = pl.ds(pl.multiple_of(t * PATHS + r, CHUNK), CHUNK)
            cg = carry[here, :] + stage[here, :]
            pc = cg * coef_a[out, :]
            parts = [cg * coef_b[out, :], pc * coef_g[out, :], pc, pc * coef_r[out, :]]
            rounded = jnp.concatenate([part.astype(BF16) for part in parts], axis=1)
            pre[out, :] = rounded
            back = lax.dot_general(rounded, w_big[...], NT, preferred_element_type=F32)
            grads[out, :] = back[:, :WIDTH]
            carry[here, :] = cg * coef_u[out, :] + back[:, WIDTH:]
            return 0

        lax.fori_loop(0, PATHS // CHUNK, chunk, 0)
        return 0

    lax.fori_loop(0, HOPS, backward_hop, 0)

    def give(o, g):
        p = o * GRP + g
        for first in range(0, CAP, 24):
            got = [grads[pl.ds(pos_s[p * 128 + first + j], 1), :] for j in range(24)]
            for j in range(24):
                stage[pl.ds(first + j, 1), :] = got[j]
        out_send[p] = stage[:CAP, :].astype(BF16)

    def give_group(i, _):
        o = ahead(i)
        for q in range(GRP):
            give(o, grps[q])
            send(out_send.at[o * GRP + grps[q]], out_recv.at[me], out_ss, out_rs.at[me_o], o, grps[q])
        return 0

    def rows8(ref, n):
        return ref.at[pl.ds(pl.multiple_of(n * 8, 8), 8), :]

    core = lax.rem(me_o, 2)
    chip = me_o // 2
    seat = chip * GRP + me_g
    half = DEV // 2
    mine = pl.ds(pl.multiple_of(core * half * 8, 8), half * 8)
    theirs = pl.ds(pl.multiple_of((1 - core) * half * 8, 8), half * 8)
    twin = me_o + 1 - 2 * core

    def to_same_core(act):
        for q in range(1, GRP):
            act(chip, grps[q])

        def body(i, _):
            z = lax.rem(chip + lax.rem(i * 5, OUTER // 2), OUTER // 2)
            for q in range(GRP):
                act(z, grps[q])
            return 0

        lax.fori_loop(1, OUTER // 2, body, 0)

    lax.fori_loop(1, 4, give_group, 0)
    w_sum[...] = jnp.zeros_like(w_sum)

    def weights(c, sums):
        rows = pl.ds(pl.multiple_of(c * PATHS, PATHS), PATHS)
        w_sum[...] += lax.dot_general(xh[rows, :], pre[rows, :], TN, preferred_element_type=F32)
        return sums + jnp.sum(pre[rows, :].astype(F32), axis=0, keepdims=True)

    sums = lax.fori_loop(0, HOPS, weights, jnp.zeros((1, 4 * WIDTH), F32))

    w_rows = [w_sum[:WIDTH, r * WIDTH : (r + 1) * WIDTH] for r in (0, 1, 2)]
    w_rows += [w_sum[WIDTH:, r * WIDTH : (r + 1) * WIDTH] for r in (0, 1, 3)]
    for r in range(6):
        w_part[pl.ds(r, DEV, stride=8), :] = w_rows[r]
    bias8 = jnp.concatenate(
        [sums[:, r * WIDTH : (r + 1) * WIDTH] for r in (0, 1, 2, 0, 1, 3)]
        + [jnp.zeros((2, WIDTH), F32)],
        axis=0,
    )
    w_part[pl.ds(6, DEV, stride=8), :] = jnp.concatenate([bias8] * (DEV // 8), axis=0)
    w_part[pl.ds(7, DEV, stride=8), :] = jnp.zeros((DEV, WIDTH), F32)
    send(w_part.at[theirs, :], w_pair, pair_s.at[0], pair_s.at[1], twin, me_g)
    lax.fori_loop(4, 7, give_group, 0)
    done(w_pair, pair_s.at[1])
    w_pair[...] += w_part[mine, :]
    to_same_core(
        lambda z, g: send(
            rows8(w_pair, z * GRP + g), rows8(w_recv, seat), w1_ss, w1_rs, z * 2 + core, g
        )
    )
    lax.fori_loop(7, 16, give_group, 0)
    done(w_recv.at[pl.ds(0, (half - 1) * 8)], w1_rs)
    own_rows = pl.ds(pl.multiple_of(seat * 8, 8), 8)
    w_recv[own_rows, :] = w_pair[own_rows, :]
    total = jnp.sum(w_recv[...].reshape(half, 8, WIDTH), axis=0)
    total = total * (1.0 / math.sqrt(ROWS * DEV))
    w_total[...] = total.astype(BF16)
    line = core * half + seat
    to_same_core(
        lambda z, g: send(w_total, all_b.at[line], w2_ss, w2_rs, z * 2 + core, g)
    )
    all_b[line] = w_total[...]
    lax.fori_loop(16, OUTER, give_group, 0)
    for q in range(1, GRP):
        give(me_o, grps[q])
        send(out_send.at[me_o * GRP + grps[q]], out_recv.at[me], out_ss, out_rs.at[me_o], me_o, grps[q])
    give(me_o, me_g)
    out_recv[me] = out_send[me]
    path_out[...] = carry[...].astype(BF16)

    link_out[...] = jnp.zeros_like(link_out)

    def collect(o):
        part = jnp.zeros((LINKS, WIDTH), F32)
        for g in range(GRP):
            p = o * GRP + g
            hot = jnp.where(iota((LINKS, 128), 0) == ask_recv[p] - 1, 1.0, 0.0).astype(BF16)
            part += jnp.dot(hot[:, :CAP], out_recv[p], preferred_element_type=F32)
        link_out[...] += part

    def collect_next(i, _):
        o = behind(i)
        done(out_recv.at[pl.ds(o * GRP, GRP)], out_rs.at[o])
        collect(o)
        return 0

    lax.fori_loop(1, OUTER // 2, collect_next, 0)
    done(all_b.at[pl.ds(0, half - 1)], w2_rs)
    send(all_b.at[pl.ds(core * half, half)], all_b.at[pl.ds(core * half, half)], pair_s.at[2], pair_s.at[3], twin, me_g)
    lax.fori_loop(OUTER // 2, OUTER, collect_next, 0)
    done(out_recv.at[pl.ds(0, GRP - 1)], out_rs.at[me_o])
    collect(me_o)
    done(all_b.at[pl.ds((1 - core) * half, half)], pair_s.at[3])
    w_all[: DEV * 8, :] = all_b[...].astype(F32).reshape(DEV * 8, WIDTH)
    for r in range(3):
        lanes = slice(r * WIDTH, (r + 1) * WIDTH)
        w_in_out[:, lanes] = w_all[pl.ds(r, DEV, stride=8), :]
        w_rec_out[:, lanes] = w_all[pl.ds(3 + r, DEV, stride=8), :]
    bias_out[...] = w_all[pl.ds(6, 8, stride=8), :]

    for buf, sem in (
        (ask_send, ask_ss), (x_send, x_ss), (agg_send, agg_ss), (out_send, out_ss)
    ):
        done(buf.at[pl.ds(0, DEV - 1)], sem)
    done(w_recv.at[pl.ds(0, (half - 1) * 8)], w1_ss)
    done(all_b.at[pl.ds(0, half - 1)], w2_ss)
    done(w_pair, pair_s.at[0])
    done(all_b.at[pl.ds(0, half)], pair_s.at[2])


def finish(path, link, w_in, w_rec, bias, path_out, link_out, w_in_out, w_rec_out, b_in_out, b_rec_out):
    path_out[...] = path[...]
    link_out[...] = link[...]
    w_in_out[...] = w_in[...]
    w_rec_out[...] = w_rec[...]
    for r in range(3):
        b_in_out[pl.ds(r * WIDTH, WIDTH)] = bias[r, :]
        b_rec_out[pl.ds(r * WIDTH, WIDTH)] = bias[3 + r, :]


def per_device(link_ids, path_states, final_grad, link_states, agg_grad, w_in, w_rec, b_in, b_rec):
    vmem = pl.BlockSpec(memory_space=pltpu.VMEM)
    one = pltpu.SemaphoreType.DMA
    some = pltpu.SemaphoreType.DMA((OUTER,))
    rows_pair = pltpu.VMEM((DEV, CAP, WIDTH), BF16)
    wide = pltpu.VMEM((ROWS, WIDTH), F32)
    shapes = (
        jax.ShapeDtypeStruct((PATHS, WIDTH), BF16),
        jax.ShapeDtypeStruct((LINKS, WIDTH), F32),
        jax.ShapeDtypeStruct((WIDTH, 3 * WIDTH), F32),
        jax.ShapeDtypeStruct((WIDTH, 3 * WIDTH), F32),
    )
    results = pl.pallas_call(
        kernel,
        out_shape=shapes + (jax.ShapeDtypeStruct((8, WIDTH), F32),),
        in_specs=[vmem] * 9,
        out_specs=(vmem,) * 5,
        scratch_shapes=[
            pltpu.VMEM((PATHS, PATHS), BF16),
            pltpu.VMEM((HOPS, PATHS), I32),
            pltpu.VMEM((ROWS,), I32),
            pltpu.VMEM((DEV, 512), F32),
            pltpu.VMEM((DEV, 128), I32),
            pltpu.VMEM((DEV, 128), I32),
            pltpu.VMEM((DEV, 1, 128), I32),
            pltpu.VMEM((DEV, 1, 128), I32),
            pltpu.VMEM((128, DEV), F32),
            pltpu.VMEM((DEV * 128,), I32),
            pltpu.SMEM((ROWS,), I32),
            pltpu.SMEM((DEV * 128,), I32),
            pltpu.VMEM((LINKS, 2 * WIDTH), BF16),
            rows_pair, rows_pair, rows_pair, rows_pair, rows_pair, rows_pair,
            pltpu.VMEM((DEV * CAP, WIDTH), F32),
            pltpu.VMEM((ROWS + 8, WIDTH), F32),
            pltpu.VMEM((PATHS, WIDTH), F32),
            wide, wide, wide, wide, wide,
            pltpu.VMEM((ROWS, 2 * WIDTH), BF16),
            pltpu.VMEM((ROWS, 4 * WIDTH), BF16),
            pltpu.VMEM((PATHS, WIDTH), F32),
            pltpu.VMEM((2 * WIDTH, 4 * WIDTH), BF16),
            pltpu.VMEM((2 * WIDTH, 4 * WIDTH), F32),
            pltpu.VMEM((DEV * 8 + 8, WIDTH), F32),
            pltpu.VMEM((DEV * 4, WIDTH), F32),
            pltpu.VMEM((DEV * 4, WIDTH), F32),
            pltpu.VMEM((8, WIDTH), BF16),
            pltpu.VMEM((DEV * 8 + 8, WIDTH), F32),
            pltpu.VMEM((DEV, 8, WIDTH), BF16),
        ] + [one, one, one, some, one, some, one, some, one, one, one, one]
        + [pltpu.SemaphoreType.DMA((4,)), pltpu.SemaphoreType.DMA((2,))],
        compiler_params=pltpu.CompilerParams(
            collective_id=0, has_side_effects=True, vmem_limit_bytes=60 * 2**20
        ),
    )(
        jnp.transpose(link_ids), path_states, final_grad, link_states, agg_grad, w_in, w_rec,
        b_in, b_rec,
    )
    flat = jax.ShapeDtypeStruct((3 * WIDTH,), F32)
    return pl.pallas_call(
        finish,
        out_shape=shapes + (flat, flat),
        in_specs=[vmem] * 5,
        out_specs=(vmem,) * 6,
    )(*results)


def solution(mesh):
    rows = P(("outer", "grp"), None)
    return jax.shard_map(
        per_device,
        mesh=mesh,
        in_specs=(rows, P(("outer", "grp"), None, None), rows, rows, rows, P(), P(), P(), P()),
        out_specs=(rows, rows, P(), P(), P(), P()),
        check_vma=False,
    )
```
